32 devices in a mesh: dp: 8 (over z, x), seq: 4 (over y, core).
Axes of the slice: x: 2, y: 2, z: 4, core: 2. Of those that a mesh axis runs over, the one named last changes fastest.
Arguments:
- tokens: bfloat16 [8, 2048, 2048], P('dp', 'seq'), may hold values from -60 to 60
- in_gain: float32 [2048], replicated, may hold values from 0.1 to 1.9
- in_weight: bfloat16 [2048, 2304], P('dp'), may hold values from -0.125 to 0.125
- conv_weight: float32 [4, 2304], replicated, may hold values from -5 to 5
- conv_bias: float32 [2304], replicated, may hold values from -3 to 3
- log_decay: float32 [8, 32, 2048], P('dp', None, 'seq'), may hold values from -0.9 to 0
- skip: float32 [32], replicated, may hold values from 0.05 to 1
- out_gain: float32 [2048], replicated, may hold values from 0.1 to 1.9
- scan_order: int32 [512], replicated, may hold values from 0 to 511, each once
Outputs:
- regrouped: bfloat16 [8, 2048, 2048], P('dp', 'seq')
The draws below stay inside these ranges and needn't reach their ends.
Inputs may be any that keep to these rules, and one draw needn't show every extreme that they name: Each of the 512 positions appears once; the q-th position of a frame in the next layer's scan is scan_order[q].
All inputs are finite; a program needn't handle non-finite values.
Results may differ from the reference program's by a relative error of at most 0.008.
Values may be sent and summed in bfloat16 or wider, within the bound.
A program may use at most 128 MiB of HBM per device.

```python
import math
import jax
import jax.numpy as jnp
from jax import lax

D = 2048
HALF_HEADS = 32
HEADDIM = 64
STATE = 128
KERNEL = 4
GROUP = 128
POSITIONS = 512
DIN = 2048
XBC = 2304
FRAMES = 4
VIDEO_LENGTH = 2048
VIDEO_COUNT = 8


def draw_tokens(key, part):
    random_keys = jax.random.split(jax.random.fold_in(key, 11), 3)
    base = jax.random.normal(random_keys[0], (VIDEO_COUNT, VIDEO_LENGTH, D), jnp.float32)
    column_scale = jnp.exp(jax.random.uniform(random_keys[1], (D,), jnp.float32, 0.0, math.log(10.0))) / 3.0
    row_scale = jnp.exp(jax.random.uniform(random_keys[2], (VIDEO_COUNT, VIDEO_LENGTH, 1), jnp.float32, 0.0, math.log(10.0))) / 3.0
    values = base * row_scale * column_scale
    return jnp.clip(values, -60.0, 60.0).astype(jnp.bfloat16)


def draw_conv_weight(key, part):
    random_keys = jax.random.split(jax.random.fold_in(key, 23), 2)
    channel_scale = 0.5 * jnp.exp(jax.random.uniform(random_keys[1], (1, XBC), jnp.float32, math.log(0.3), math.log(3.0)))
    base = jax.random.normal(random_keys[0], (KERNEL, XBC), jnp.float32)
    return jnp.clip(base * channel_scale, -5.0, 5.0)


def draw_log_decay(key, part):
    random_keys = jax.random.split(jax.random.fold_in(key, 37), 7)
    share = 0.5
    slow_heads = jax.random.uniform(random_keys[0], (VIDEO_COUNT, HALF_HEADS, 1), jnp.float32) < share
    slow_rate = math.log(10.0) * jax.random.uniform(random_keys[1], (VIDEO_COUNT, HALF_HEADS, 1), jnp.float32, 0.1, 0.3) / VIDEO_LENGTH
    fast_rate = jnp.exp(jax.random.uniform(random_keys[2], (VIDEO_COUNT, HALF_HEADS, 1), jnp.float32, math.log(1.0 / 50.0), math.log(1.0 / 30.0)))
    base_rate = jnp.where(slow_heads, slow_rate, fast_rate)
    frame_count = VIDEO_LENGTH // POSITIONS
    frame_factor = jnp.exp(jax.random.uniform(random_keys[3], (VIDEO_COUNT, HALF_HEADS, frame_count, 1), jnp.float32, math.log(0.5), math.log(2.0)))
    frame_factor = jnp.broadcast_to(frame_factor, (VIDEO_COUNT, HALF_HEADS, frame_count, POSITIONS)).reshape(VIDEO_COUNT, HALF_HEADS, VIDEO_LENGTH)
    token_factor = jnp.exp(jax.random.uniform(random_keys[4], (VIDEO_COUNT, HALF_HEADS, VIDEO_LENGTH), jnp.float32, math.log(0.5), math.log(2.0)))
    decay_rate = base_rate * frame_factor * token_factor
    spike_positions = jax.random.randint(random_keys[5], (VIDEO_COUNT, 2), 0, VIDEO_LENGTH)
    spike_reached = jnp.any(jnp.arange(VIDEO_LENGTH)[None, None, :] == spike_positions[:, :, None], axis=1)
    spike_penalty = jax.random.uniform(random_keys[6], (VIDEO_COUNT, HALF_HEADS, VIDEO_LENGTH), jnp.float32, 0.2, 0.5)
    return -decay_rate + jnp.where(spike_reached[:, None, :], jnp.log1p(-spike_penalty), 0.0)


def level_of(stream_key, dims, shards, low, high):
    def one(position, blocks):
        draws = jax.random.uniform(jax.random.fold_in(jax.random.fold_in(stream_key, 6), position), (blocks,), jnp.float32, low / len(shards), high / len(shards))
        return jnp.repeat(jnp.exp(draws), dims[position] // blocks).reshape((-1,) + (1,) * (len(dims) - position - 1))

    level = one(*shards[0])
    for cut in shards[1:]:
        level = level * one(*cut)
    return level


def noise(rng, extent, deviation, bound, cuts=(), held_as=jnp.bfloat16):
    result = deviation * jax.random.normal(rng, extent, jnp.float32)
    if cuts:
        result = result * level_of(rng, extent, cuts, -0.22, 0.18)
    return jnp.clip(result, -bound, bound).astype(held_as)


def setup_inputs(seed: int = 0) -> dict:
    splits = jax.random.split(jax.random.key(seed), 10)
    tokens = draw_tokens(jax.random.fold_in(splits[9], 71), 0)
    in_gain = jnp.clip(1.0 + 0.18 * jax.random.normal(splits[1], (D,), jnp.float32), 0.1, 1.9)
    in_weight = noise(splits[2], (D, XBC), D ** -0.5, 0.125, ((0, 8),))
    conv_weight = draw_conv_weight(jax.random.fold_in(splits[9], 71), 0)
    conv_bias = noise(splits[4], (XBC,), 0.5, 3.0, (), jnp.float32)
    log_decay = draw_log_decay(jax.random.fold_in(splits[9], 71), 0)
    skip = jnp.clip(jnp.exp(jax.random.uniform(splits[6], (HALF_HEADS,), jnp.float32, math.log(0.05), math.log(1.0))), 0.05, 1.0)
    out_gain = jnp.clip(1.0 + 0.18 * jax.random.normal(splits[7], (DIN,), jnp.float32), 0.1, 1.9)
    scan_order = jax.random.permutation(splits[8], POSITIONS).astype(jnp.int32)
    return {"tokens": tokens, "in_gain": in_gain, "in_weight": in_weight, "conv_weight": conv_weight, "conv_bias": conv_bias, "log_decay": log_decay, "skip": skip, "out_gain": out_gain, "scan_order": scan_order}


def group_pass(x_block, b_block, c_block, decay_block, entering):
    cumulative = jnp.cumsum(decay_block, axis=1)
    step_size = -decay_block
    scores = jnp.dot(c_block, b_block.T, preferred_element_type=jnp.float32)
    log_gap = cumulative[:, :, None] - cumulative[:, None, :]
    length = decay_block.shape[1]
    causal = jnp.arange(length)[None, :] <= jnp.arange(length)[:, None]
    decay_mask = jnp.exp(jnp.where(causal[None], log_gap, -1e+30))
    weights = (scores[None] * decay_mask * step_size[:, None, :]).astype(jnp.bfloat16)
    weights = lax.optimization_barrier(weights)
    intra = jnp.einsum('hts,shp->thp', weights.astype(jnp.float32), x_block.astype(jnp.float32), precision=lax.Precision.HIGHEST)
    closing = cumulative[:, -1:]
    scaled = ((jnp.exp(closing - cumulative) * step_size).T[:, :, None] * x_block.astype(jnp.float32)).astype(jnp.bfloat16)
    scaled = lax.optimization_barrier(scaled)
    block_state = jnp.einsum('shp,sn->hpn', scaled.astype(jnp.float32), b_block.astype(jnp.float32), precision=lax.Precision.HIGHEST)
    entering_half = lax.optimization_barrier(entering.astype(jnp.bfloat16))
    inter = jnp.einsum('tn,hpn->thp', c_block.astype(jnp.float32), entering_half.astype(jnp.float32), precision=lax.Precision.HIGHEST)
    inter = inter * jnp.exp(cumulative).T[:, :, None]
    following = jnp.exp(closing[:, 0])[:, None, None] * entering + block_state
    return (intra + inter, following)

def one_video(tokens_one, decay_one, in_gain, in_weight, conv_weight, conv_bias, skip, out_gain, scan_order):
    widened = tokens_one.astype(jnp.float32)
    inverse = lax.rsqrt(lax.optimization_barrier(jnp.mean(widened * widened, axis=1, keepdims=True)) + 1e-05)
    normed = (widened * inverse * in_gain[None, :]).astype(jnp.bfloat16)
    projected = jnp.dot(normed, in_weight, preferred_element_type=jnp.float32).astype(jnp.bfloat16)
    padded = jnp.concatenate([jnp.zeros((KERNEL - 1, XBC), jnp.bfloat16), projected], axis=0)
    mixed_pre = conv_bias[None, :] + conv_weight[0][None, :] * padded[0:VIDEO_LENGTH].astype(jnp.float32)
    for offset in range(1, KERNEL):
        mixed_pre = mixed_pre + conv_weight[offset][None, :] * padded[offset:offset + VIDEO_LENGTH].astype(jnp.float32)
    mixed = jax.nn.silu(mixed_pre).astype(jnp.bfloat16)
    inner_width = HALF_HEADS * HEADDIM
    x_heads = mixed[:, :inner_width].reshape(VIDEO_LENGTH, HALF_HEADS, HEADDIM)
    b_vectors = mixed[:, inner_width:inner_width + STATE]
    c_vectors = mixed[:, inner_width + STATE:]
    block_count = VIDEO_LENGTH // GROUP

    def advance(entering, inputs):
        x_block, b_block, c_block, decay_block = inputs
        output, following = group_pass(x_block, b_block, c_block, decay_block, entering)
        return (following, output)
    inputs = (x_heads.reshape(block_count, GROUP, HALF_HEADS, HEADDIM), b_vectors.reshape(block_count, GROUP, STATE), c_vectors.reshape(block_count, GROUP, STATE), decay_one.reshape(HALF_HEADS, block_count, GROUP).transpose(1, 0, 2))
    carried, outputs = lax.scan(advance, jnp.zeros((HALF_HEADS, HEADDIM, STATE), jnp.float32), inputs)
    ssm_out = outputs.reshape(VIDEO_LENGTH, HALF_HEADS, HEADDIM) + skip[None, :, None] * x_heads.astype(jnp.float32)
    head_scale = lax.rsqrt(lax.optimization_barrier(jnp.mean(ssm_out * ssm_out, axis=2, keepdims=True)) + 1e-05)
    normalized = (ssm_out * head_scale * out_gain.reshape(HALF_HEADS, HEADDIM)[None]).astype(jnp.bfloat16)
    framed = normalized.reshape(FRAMES, POSITIONS, inner_width)
    picked = jnp.take(framed, scan_order, axis=1)
    return picked.transpose(1, 0, 2).reshape(VIDEO_LENGTH, inner_width)

def reference(tokens, in_gain, in_weight, conv_weight, conv_bias, log_decay, skip, out_gain, scan_order):

    def per_video(video_pair):
        return one_video(video_pair[0], video_pair[1], in_gain, in_weight, conv_weight, conv_bias, skip, out_gain, scan_order)
    return lax.map(per_video, (tokens, log_decay))
```

```python
import functools
import math

import jax
import jax.numpy as jnp
from jax import lax
from jax.experimental import pallas as pl
from jax.experimental.pallas import tpu as pltpu
from jax.sharding import PartitionSpec as P

GROUP = 128
CHUNK = 256
HALO = 16
BF16 = jnp.bfloat16
F32 = jnp.float32
MESH = pl.DeviceIdType.MESH


def fused_kernel(
    sizes,
    tokens_ref,
    gain_ref,
    weight_ref,
    conv_weight_ref,
    conv_bias_ref,
    decay_ref,
    lane_ref,
    order_ref,
    result_ref,
    slabs,
    normed,
    projected,
    mixed,
    b_turned,
    c_held,
    scores,
    block_states,
    entering_half,
    intra,
    expanded,
    arriving_state,
    leaving_state,
    normalized,
    picked,
    z_send,
    z_recv,
    x_send,
    x_recv,
    core_send,
    core_recv,
    halo_send,
    halo_recv,
    state_send,
    state_recv,
    out_send,
    out_recv,
    own_sem,
):
    z_count, x_count, core_count, seq_count, head_width = sizes
    head_count = CHUNK // head_width
    dp = lax.axis_index("dp")
    seq = lax.axis_index("seq")
    z = dp // x_count
    x = dp % x_count
    core = seq % core_count
    sibling = seq - core + (core + 1) % core_count
    half = slabs.shape[4]
    slab_count = slabs.shape[0]
    chunk_count = slab_count - 1
    token_count, width = tokens_ref.shape
    block_count = token_count // GROUP
    positions = order_ref.shape[0]
    share = positions // seq_count

    partners = [(((z + k) % z_count) * x_count + x, seq) for k in range(1, z_count)]
    partners += [(z * x_count + (x + k) % x_count, seq) for k in range(1, x_count)]
    partners += [(dp, (seq + k) % seq_count) for k in range(1, seq_count)]
    barrier = pltpu.get_barrier_semaphore()
    for partner in partners:
        pl.semaphore_signal(barrier, inc=1, device_id=partner, device_id_type=MESH)

    own_rows = pl.ds(pl.multiple_of(core * half, half), half)
    for slab in range(slab_count):
        first = chunk_count * CHUNK if slab == 0 else (slab - 1) * CHUNK
        slabs[slab, z, x, core] = weight_ref[own_rows, first : first + CHUNK]
    pl.semaphore_wait(barrier, len(partners))

    def z_copy(slab, k, source):
        return pltpu.make_async_remote_copy(
            src_ref=slabs.at[slab, source, x, core],
            dst_ref=slabs.at[slab, source, x, core],
            send_sem=z_send.at[slab, k - 1],
            recv_sem=z_recv.at[slab, k - 1],
            device_id=(((z + k) % z_count) * x_count + x, seq),
            device_id_type=MESH,
        )

    def x_copy(slab, k, source):
        return pltpu.make_async_remote_copy(
            src_ref=slabs.at[slab, :, source, core],
            dst_ref=slabs.at[slab, :, source, core],
            send_sem=x_send.at[slab, k - 1],
            recv_sem=x_recv.at[slab, k - 1],
            device_id=(z * x_count + (x + k) % x_count, seq),
            device_id_type=MESH,
        )

    def core_copy(slab, source):
        return pltpu.make_async_remote_copy(
            src_ref=slabs.at[slab, :, :, source],
            dst_ref=slabs.at[slab, :, :, source],
            send_sem=core_send.at[slab],
            recv_sem=core_recv.at[slab],
            device_id=(dp, sibling),
            device_id_type=MESH,
        )

    for slab in range(slab_count):
        for k in range(1, z_count):
            z_copy(slab, k, z).start()

    def pass_x(slab):
        for k in range(1, z_count):
            z_copy(slab, k, (z + z_count - k) % z_count).wait_recv()
        for k in range(1, x_count):
            x_copy(slab, k, x).start()

    def pass_core(slab):
        for k in range(1, x_count):
            x_copy(slab, k, (x + x_count - k) % x_count).wait_recv()
        if core_count > 1:
            core_copy(slab, core).start()

    def whole_slab(slab):
        if core_count > 1:
            core_copy(slab, (core + 1) % core_count).wait_recv()

    for block in range(block_count):
        rows = tokens_ref[block * GROUP : (block + 1) * GROUP, :].astype(F32)
        inverse = lax.rsqrt(jnp.mean(rows * rows, axis=1, keepdims=True) + 1e-05)
        normed[HALO + block * GROUP : HALO + (block + 1) * GROUP, :] = (
            rows * inverse * gain_ref[...]
        ).astype(BF16)

    halo_copy = pltpu.make_async_remote_copy(
        src_ref=normed.at[token_count : token_count + HALO],
        dst_ref=normed.at[0:HALO],
        send_sem=halo_send,
        recv_sem=halo_recv,
        device_id=(dp, (seq + 1) % seq_count),
        device_id_type=MESH,
    )

    @pl.when(seq < seq_count - 1)
    def _():
        halo_copy.start()

    @pl.when(seq == 0)
    def _():
        normed[0:HALO, :] = jnp.zeros((HALO, width), BF16)

    row_at = lax.broadcasted_iota(jnp.int32, (GROUP, GROUP), 0)
    column_at = lax.broadcasted_iota(jnp.int32, (GROUP, GROUP), 1)
    causal = column_at <= row_at
    lower = jnp.where(causal, 1.0, 0.0).astype(F32)
    unit = jnp.where(row_at == column_at, 1.0, 0.0).astype(F32)
    upper = jnp.where(row_at <= column_at, 1.0, 0.0).astype(F32)
    first_head = lax.broadcasted_iota(jnp.int32, (1, GROUP), 1) < head_width
    same_head = jnp.where(row_at // head_width == column_at // head_width, 1.0, 0.0).astype(BF16)
    same_head_twice = jnp.concatenate([same_head, same_head], axis=0)

    def project(slab):
        matrix = slabs[slab].reshape(width, CHUNK)
        projected[...] = (
            jnp.dot(normed[...], matrix, preferred_element_type=F32).astype(BF16).astype(F32)
        )
        taps = conv_weight_ref.shape[1]
        for block in range(block_count):
            total = conv_bias_ref[slab]
            for tap in range(taps):
                first = HALO + block * GROUP + tap - (taps - 1)
                total = total + conv_weight_ref[slab, tap : tap + 1, :] * projected[
                    first : first + GROUP, :
                ]
            mixed[block * GROUP : (block + 1) * GROUP, :] = (total / (1.0 + jnp.exp(-total))).astype(
                BF16
            )

    def both(columns, pair):
        return jnp.where(
            first_head, columns[:, 2 * pair : 2 * pair + 1], columns[:, 2 * pair + 1 : 2 * pair + 2]
        )

    pass_x(0)
    pass_x(1)
    pass_core(0)

    @pl.when(seq > 0)
    def _():
        halo_copy.wait_recv()

    whole_slab(0)
    project(0)
    for block in range(block_count):
        rows = slice(block * GROUP, (block + 1) * GROUP)
        b_block = mixed[rows, :GROUP]
        c_block = mixed[rows, GROUP:]
        c_held[block] = c_block
        b_turned[block] = jnp.transpose(b_block.astype(F32)).astype(BF16)
        scores[block] = jnp.where(
            causal, jnp.dot(c_block, b_turned[block], preferred_element_type=F32), 0.0
        )
    order = order_ref[...]
    choice = jnp.where(
        lax.broadcasted_iota(jnp.int32, (positions, positions), 1) == order, 1.0, 0.0
    ).astype(BF16)

    def state_copy(chunk):
        return pltpu.make_async_remote_copy(
            src_ref=leaving_state.at[chunk],
            dst_ref=arriving_state.at[chunk],
            send_sem=state_send.at[chunk],
            recv_sem=state_recv.at[chunk],
            device_id=(dp, (seq + 1) % seq_count),
            device_id_type=MESH,
        )

    def out_columns(chunk):
        return pl.ds(pl.multiple_of(chunk * CHUNK, CHUNK), CHUNK)

    def work(chunk, carry):
        slab = chunk + 1

        @pl.when(slab + 1 < slab_count)
        def _():
            pass_x(slab + 1)

        pass_core(slab)
        whole_slab(slab)
        project(slab)
        fadings = []
        for block in range(block_count):
            rows = slice(block * GROUP, (block + 1) * GROUP)
            decay = decay_ref[chunk, :, rows]
            across = jnp.dot(decay, upper, precision=lax.Precision.HIGHEST, preferred_element_type=F32)
            down = lax.dot_general(
                lower,
                decay,
                (((1,), (1,)), ((), ())),
                precision=lax.Precision.HIGHEST,
                preferred_element_type=F32,
            )
            down_decay = lax.dot_general(
                unit,
                decay,
                (((1,), (1,)), ((), ())),
                precision=lax.Precision.HIGHEST,
                preferred_element_type=F32,
            )
            closing = down[GROUP - 1 : GROUP, :]
            scale = jnp.exp(closing - down) * (-down_decay)
            fading = jnp.exp(closing)
            grown = jnp.exp(down)
            fades = []
            for pair in range(head_count // 2):
                lanes = slice(pair * GROUP, (pair + 1) * GROUP)
                x_pair = mixed[rows, lanes]
                parts = []
                for head in (2 * pair, 2 * pair + 1):
                    gap = down[:, head : head + 1] - across[head : head + 1, :]
                    weights = (
                        scores[block]
                        * jnp.exp(jnp.minimum(gap, 0.0))
                        * (-decay[head : head + 1, :])
                    ).astype(BF16)
                    parts.append(jnp.dot(weights, x_pair, preferred_element_type=F32))
                x_wide = x_pair.astype(F32)
                intra[rows, lanes] = (
                    jnp.where(first_head, parts[0], parts[1])
                    + lane_ref[chunk, 0:1, lanes] * x_wide
                )
                scaled = (both(scale, pair) * x_wide).astype(BF16)
                block_states[block, :, lanes] = jnp.dot(
                    b_turned[block], scaled, preferred_element_type=F32
                )
                expanded[rows, lanes] = both(grown, pair)
                fades.append(both(fading, pair))
            fadings.append(jnp.concatenate(fades, axis=1))

        @pl.when(seq > 0)
        def _():
            state_copy(chunk).wait_recv()

        @pl.when(seq == 0)
        def _():
            arriving_state[chunk] = jnp.zeros(arriving_state.shape[1:], F32)

        state = arriving_state[chunk]
        for block in range(block_count):
            entering_half[block] = state.astype(BF16)
            state = fadings[block] * state + block_states[block]
        leaving_state[chunk] = state

        @pl.when(seq < seq_count - 1)
        def _():
            state_copy(chunk).start()

        for block in range(block_count):
            rows = slice(block * GROUP, (block + 1) * GROUP)
            inter = jnp.dot(c_held[block], entering_half[block], preferred_element_type=F32)
            ssm = intra[rows, :] + inter * expanded[rows, :]
            square = ssm * ssm
            high = square.astype(BF16)
            low = (square - high.astype(F32)).astype(BF16)
            for pair in range(head_count // 2):
                lanes = slice(pair * GROUP, (pair + 1) * GROUP)
                total = jnp.dot(
                    jnp.concatenate([high[:, lanes], low[:, lanes]], axis=1),
                    same_head_twice,
                    preferred_element_type=F32,
                )
                head_scale = lax.rsqrt(total * (1.0 / head_width) + 1e-05)
                normalized[rows, lanes] = (
                    ssm[:, lanes] * head_scale * lane_ref[chunk, 1:2, lanes]
                ).astype(BF16)
        picked[chunk] = jnp.dot(choice, normalized[...], preferred_element_type=F32).astype(BF16)
        for k in range(1, seq_count):
            target = (seq + k) % seq_count
            pltpu.make_async_remote_copy(
                src_ref=picked.at[chunk, pl.ds(pl.multiple_of(target * share, share), share)],
                dst_ref=result_ref.at[seq, :, out_columns(chunk)],
                send_sem=out_send.at[k - 1],
                recv_sem=out_recv.at[k - 1],
                device_id=(dp, target),
                device_id_type=MESH,
            ).start()
        pltpu.make_async_copy(
            picked.at[chunk, pl.ds(pl.multiple_of(seq * share, share), share)],
            result_ref.at[seq, :, out_columns(chunk)],
            own_sem,
        ).start()
        return carry

    lax.fori_loop(0, chunk_count, work, 0)

    for k in range(1, seq_count):
        source = (seq + seq_count - k) % seq_count
        whole = pltpu.make_async_remote_copy(
            src_ref=result_ref.at[source],
            dst_ref=result_ref.at[source],
            send_sem=out_send.at[k - 1],
            recv_sem=out_recv.at[k - 1],
            device_id=(dp, (seq + k) % seq_count),
            device_id_type=MESH,
        )
        whole.wait_recv()
        whole.wait_send()
    pltpu.make_async_copy(result_ref.at[seq], result_ref.at[seq], own_sem).wait()

    def settle(slab, carry):
        for k in range(1, z_count):
            z_copy(slab, k, z).wait_send()
        for k in range(1, x_count):
            x_copy(slab, k, x).wait_send()
        if core_count > 1:
            core_copy(slab, core).wait_send()
        return carry

    lax.fori_loop(0, slab_count, settle, 0)

    @pl.when(seq < seq_count - 1)
    def _():
        halo_copy.wait_send()

        def state_settle(chunk, carry):
            state_copy(chunk).wait_send()
            return carry

        lax.fori_loop(0, chunk_count, state_settle, 0)


def interleave_kernel(frame_count, arrived_ref, out_ref):
    rows = arrived_ref.shape[0]
    share = rows // frame_count
    row = lax.broadcasted_iota(jnp.int32, (rows, rows), 0)
    column = lax.broadcasted_iota(jnp.int32, (rows, rows), 1)
    choice = jnp.where(
        column == (row % frame_count) * share + row // frame_count, 1.0, 0.0
    ).astype(BF16)
    out_ref[...] = jnp.dot(choice, arrived_ref[...], preferred_element_type=F32).astype(BF16)


def on_device(
    sizes, tokens, in_gain, in_weight, conv_weight, conv_bias, log_decay, skip, out_gain, scan_order
):
    z_count, x_count, core_count, seq_count = sizes
    token_count, width = tokens.shape[1:]
    own_rows, channels = in_weight.shape
    heads = log_decay.shape[1]
    inner = out_gain.shape[0]
    head_width = inner // heads
    chunk_count = inner // CHUNK
    slab_count = chunk_count + 1
    per_chunk = heads // chunk_count
    taps = conv_weight.shape[0]
    positions = scan_order.shape[0]
    share = positions // seq_count
    assert token_count == positions and channels == inner + 2 * GROUP and per_chunk == 4

    def by_slab(rows):
        split = rows.reshape(rows.shape[0], slab_count, CHUNK).transpose(1, 0, 2)
        return jnp.concatenate([split[-1:], split[:-1]], axis=0)

    decay = log_decay[0].reshape(chunk_count, per_chunk, token_count)
    decay = jnp.pad(decay, ((0, 0), (0, 8 - per_chunk), (0, 0)))
    lane_skip = jnp.repeat(skip, head_width).reshape(chunk_count, 1, CHUNK)
    lane_gain = out_gain.reshape(chunk_count, 1, CHUNK)
    vmem = pl.BlockSpec(memory_space=pltpu.VMEM)
    hops = max(z_count - 1, 1), max(x_count - 1, 1), max(seq_count - 1, 1)
    arrived = pl.pallas_call(
        functools.partial(fused_kernel, sizes + (head_width,)),
        out_shape=jax.ShapeDtypeStruct((seq_count, share, inner), BF16),
        in_specs=[vmem] * 8,
        out_specs=pl.BlockSpec(memory_space=pl.ANY),
        scratch_shapes=[
            pltpu.VMEM(
                (slab_count, z_count, x_count, core_count, own_rows // core_count, CHUNK), BF16
            ),
            pltpu.VMEM((HALO + token_count, width), BF16),
            pltpu.VMEM((HALO + token_count, CHUNK), F32),
            pltpu.VMEM((token_count, CHUNK), BF16),
            pltpu.VMEM((token_count // GROUP, GROUP, GROUP), BF16),
            pltpu.VMEM((token_count // GROUP, GROUP, GROUP), BF16),
            pltpu.VMEM((token_count // GROUP, GROUP, GROUP), F32),
            pltpu.VMEM((token_count // GROUP, GROUP, CHUNK), F32),
            pltpu.VMEM((token_count // GROUP, GROUP, CHUNK), BF16),
            pltpu.VMEM((token_count, CHUNK), F32),
            pltpu.VMEM((token_count, CHUNK), F32),
            pltpu.VMEM((chunk_count, GROUP, CHUNK), F32),
            pltpu.VMEM((chunk_count, GROUP, CHUNK), F32),
            pltpu.VMEM((token_count, CHUNK), BF16),
            pltpu.VMEM((chunk_count, positions, CHUNK), BF16),
            pltpu.SemaphoreType.DMA((slab_count, hops[0])),
            pltpu.SemaphoreType.DMA((slab_count, hops[0])),
            pltpu.SemaphoreType.DMA((slab_count, hops[1])),
            pltpu.SemaphoreType.DMA((slab_count, hops[1])),
            pltpu.SemaphoreType.DMA((slab_count,)),
            pltpu.SemaphoreType.DMA((slab_count,)),
            pltpu.SemaphoreType.DMA,
            pltpu.SemaphoreType.DMA,
            pltpu.SemaphoreType.DMA((chunk_count,)),
            pltpu.SemaphoreType.DMA((chunk_count,)),
            pltpu.SemaphoreType.DMA((hops[2],)),
            pltpu.SemaphoreType.DMA((hops[2],)),
            pltpu.SemaphoreType.DMA,
        ],
        compiler_params=pltpu.CompilerParams(
            collective_id=0, has_side_effects=True, vmem_limit_bytes=52 * 1024 * 1024
        ),
        name="projected_scan",
    )(
        tokens[0],
        in_gain.reshape(1, width),
        in_weight,
        by_slab(conv_weight),
        by_slab(conv_bias.reshape(1, channels)),
        decay,
        jnp.concatenate([lane_skip, lane_gain], axis=1),
        scan_order.reshape(positions, 1),
    )
    columns = min(512, inner)
    out = pl.pallas_call(
        functools.partial(interleave_kernel, seq_count),
        out_shape=jax.ShapeDtypeStruct((token_count, inner), BF16),
        grid=(inner // columns,),
        in_specs=[pl.BlockSpec((token_count, columns), lambda i: (0, i))],
        out_specs=pl.BlockSpec((token_count, columns), lambda i: (0, i)),
        name="frames_within_positions",
    )(arrived.reshape(token_count, inner))
    return out[None]


def solution(mesh):
    dp_count, seq_count = mesh.shape["dp"], mesh.shape["seq"]
    x_count = 2 ** (int(math.log2(dp_count)) // 2)
    while dp_count % x_count:
        x_count //= 2
    sizes = (dp_count // x_count, x_count, 2 if seq_count % 2 == 0 else 1, seq_count)
    in_specs = (
        P("dp", "seq", None),
        P(),
        P("dp", None),
        P(),
        P(),
        P("dp", None, "seq"),
        P(),
        P(),
        P(),
    )
    return jax.shard_map(
        functools.partial(on_device, sizes),
        mesh=mesh,
        in_specs=in_specs,
        out_specs=P("dp", "seq", None),
        check_vma=False,
    )
```

```python
import functools
import math

import jax
import jax.numpy as jnp
from jax import lax
from jax.experimental import pallas as pl
from jax.experimental.pallas import tpu as pltpu
from jax.sharding import PartitionSpec as P

GROUP = 128
CHUNK = 256
HALO = 16
WINDOW = 3
BF16 = jnp.bfloat16
F32 = jnp.float32
MESH = pl.DeviceIdType.MESH


def fused_kernel(
    sizes,
    tokens_hbm,
    gain_ref,
    weight_hbm,
    conv_weight_ref,
    conv_bias_ref,
    decay_ref,
    skip_ref,
    out_gain_ref,
    order_ref,
    result_ref,
    tokens_ref,
    slabs,
    normed,
    choice,
    down_held,
    down_decay_held,
    across_held,
    decay_held,
    projected,
    mixed,
    b_turned,
    c_held,
    scores,
    block_states,
    entering_half,
    intra,
    expanded,
    arriving_state,
    leaving_state,
    normalized,
    picked,
    z_send,
    z_recv,
    x_send,
    x_recv,
    core_send,
    core_recv,
    halo_send,
    halo_recv,
    state_send,
    state_recv,
    out_send,
    out_recv,
    own_sem,
    token_sem,
    weight_sem,
):
    z_count, x_count, core_count, seq_count, head_width = sizes
    head_count = CHUNK // head_width
    dp = lax.axis_index("dp")
    seq = lax.axis_index("seq")
    z = dp // x_count
    x = dp % x_count
    core = seq % core_count
    sibling = seq - core + (core + 1) % core_count
    half = slabs.shape[4]
    slab_count = slabs.shape[0]
    chunk_count = slab_count - 1
    token_count, width = tokens_ref.shape
    block_count = token_count // GROUP
    positions = order_ref.shape[1]
    share = positions // seq_count

    partners = [(((z + k) % z_count) * x_count + x, seq) for k in range(1, z_count)]
    partners += [(z * x_count + (x + k) % x_count, seq) for k in range(1, x_count)]
    partners += [(dp, (seq + k) % seq_count) for k in range(1, seq_count)]
    barrier = pltpu.get_barrier_semaphore()
    for partner in partners:
        pl.semaphore_signal(barrier, inc=1, device_id=partner, device_id_type=MESH)

    own_rows = pl.ds(pl.multiple_of(core * half, half), half)

    def load_weight(slab):
        first = chunk_count * CHUNK if slab == 0 else (slab - 1) * CHUNK
        return pltpu.make_async_copy(
            weight_hbm.at[own_rows, first : first + CHUNK],
            slabs.at[slab, z, x, core],
            weight_sem.at[slab],
        )

    def load_tokens(block):
        rows = slice(block * GROUP, (block + 1) * GROUP)
        return pltpu.make_async_copy(tokens_hbm.at[rows], tokens_ref.at[rows], token_sem.at[block])

    for slab in range(slab_count):
        load_weight(slab).start()
    for block in range(block_count):
        load_tokens(block).start()
    for slab in range(slab_count):
        load_weight(slab).wait()
    pl.semaphore_wait(barrier, len(partners))

    def z_copy(slab, k, source):
        return pltpu.make_async_remote_copy(
            src_ref=slabs.at[slab, source, x, core],
            dst_ref=slabs.at[slab, source, x, core],
            send_sem=z_send.at[slab, k - 1],
            recv_sem=z_recv.at[slab, k - 1],
            device_id=(((z + k) % z_count) * x_count + x, seq),
            device_id_type=MESH,
        )

    def x_copy(slab, k, source, row):
        piece = slabs.at[slab, row, source, core]
        return pltpu.make_async_remote_copy(
            src_ref=piece,
            dst_ref=piece,
            send_sem=x_send.at[slab, k - 1],
            recv_sem=x_recv.at[slab, k - 1],
            device_id=(z * x_count + (x + k) % x_count, seq),
            device_id_type=MESH,
        )

    def core_copy(slab, source):
        return pltpu.make_async_remote_copy(
            src_ref=slabs.at[slab, :, :, source],
            dst_ref=slabs.at[slab, :, :, source],
            send_sem=core_send.at[slab],
            recv_sem=core_recv.at[slab],
            device_id=(dp, sibling),
            device_id_type=MESH,
        )

    def send_own(slab):
        for k in range(1, z_count):
            z_copy(slab, k, z).start()
        for k in range(1, x_count):
            x_copy(slab, k, x, z).start()

    def pass_x(slab):
        for k in range(1, z_count):
            row = (z + z_count - k) % z_count
            z_copy(slab, k, row).wait_recv()
            for kx in range(1, x_count):
                x_copy(slab, kx, x, row).start()

        if isinstance(slab, int):
            if slab + WINDOW < slab_count:
                send_own(slab + WINDOW)
        else:

            @pl.when(slab + WINDOW < slab_count)
            def _():
                send_own(slab + WINDOW)

    def pass_core(slab):
        for k in range(1, x_count):
            x_copy(slab, k, (x + x_count - k) % x_count, slice(None)).wait_recv()
        if core_count > 1:
            core_copy(slab, core).start()

    def whole_slab(slab):
        if core_count > 1:
            core_copy(slab, (core + 1) % core_count).wait_recv()

    for slab in range(min(WINDOW, slab_count)):
        send_own(slab)

    for block in range(block_count):
        load_tokens(block).wait()
        rows = tokens_ref[block * GROUP : (block + 1) * GROUP, :].astype(F32)
        inverse = lax.rsqrt(jnp.mean(rows * rows, axis=1, keepdims=True) + 1e-05)
        normed[HALO + block * GROUP : HALO + (block + 1) * GROUP, :] = (
            rows * inverse * gain_ref[...]
        ).astype(BF16)

    halo_copy = pltpu.make_async_remote_copy(
        src_ref=normed.at[token_count : token_count + HALO],
        dst_ref=normed.at[0:HALO],
        send_sem=halo_send,
        recv_sem=halo_recv,
        device_id=(dp, (seq + 1) % seq_count),
        device_id_type=MESH,
    )

    @pl.when(seq < seq_count - 1)
    def _():
        halo_copy.start()

    @pl.when(seq == 0)
    def _():
        normed[0:HALO, :] = jnp.zeros((HALO, width), BF16)

    row_at = lax.broadcasted_iota(jnp.int32, (GROUP, GROUP), 0)
    column_at = lax.broadcasted_iota(jnp.int32, (GROUP, GROUP), 1)
    causal = column_at <= row_at
    lower = jnp.where(causal, 1.0, 0.0).astype(F32)
    unit = jnp.where(row_at == column_at, 1.0, 0.0).astype(F32)
    upper = jnp.where(row_at <= column_at, 1.0, 0.0).astype(F32)
    first_head = lax.broadcasted_iota(jnp.int32, (1, GROUP), 1) < head_width
    same_head = jnp.where(row_at // head_width == column_at // head_width, 1.0, 0.0).astype(BF16)
    same_head_twice = jnp.concatenate([same_head, same_head], axis=0)

    def project(slab, first_column):
        columns = pl.ds(first_column, CHUNK)
        matrix = slabs[slab].reshape(width, CHUNK)
        projected[...] = (
            jnp.dot(normed[...], matrix, preferred_element_type=F32).astype(BF16).astype(F32)
        )
        taps = conv_weight_ref.shape[0]
        for block in range(block_count):
            total = conv_bias_ref[:, columns]
            for tap in range(taps):
                first = HALO + block * GROUP + tap - (taps - 1)
                total = total + conv_weight_ref[tap : tap + 1, columns] * projected[
                    first : first + GROUP, :
                ]
            mixed[block * GROUP : (block + 1) * GROUP, :] = (total / (1.0 + jnp.exp(-total))).astype(
                BF16
            )

    def both(columns, pair):
        return jnp.where(
            first_head, columns[:, 2 * pair : 2 * pair + 1], columns[:, 2 * pair + 1 : 2 * pair + 2]
        )

    pass_x(0)
    for block in range(block_count):
        rows = slice(block * GROUP, (block + 1) * GROUP)
        decay = decay_ref[:, rows]
        across = jnp.dot(decay, upper, precision=lax.Precision.HIGHEST, preferred_element_type=F32)
        turned = (((1,), (1,)), ((), ()))
        down = lax.dot_general(
            lower, decay, turned, precision=lax.Precision.HIGHEST, preferred_element_type=F32
        )
        down_decay = lax.dot_general(
            unit, decay, turned, precision=lax.Precision.HIGHEST, preferred_element_type=F32
        )
        for chunk in range(chunk_count):
            heads = slice(chunk * head_count, (chunk + 1) * head_count)
            down_held[chunk, rows, :head_count] = down[:, heads]
            down_decay_held[chunk, rows, :head_count] = down_decay[:, heads]
            across_held[chunk, :head_count, rows] = across[heads, :]
            decay_held[chunk, :head_count, rows] = decay[heads, :]
    pass_core(0)
    pass_x(1)
    choice[...] = jnp.transpose(
        jnp.where(
            lax.broadcasted_iota(jnp.int32, (positions, positions), 0) == order_ref[...], 1.0, 0.0
        ).astype(F32)
    ).astype(BF16)

    @pl.when(seq > 0)
    def _():
        halo_copy.wait_recv()

    whole_slab(0)
    project(0, chunk_count * CHUNK)
    pass_x(2)
    pass_core(1)
    for block in range(block_count):
        rows = slice(block * GROUP, (block + 1) * GROUP)
        b_block = mixed[rows, :GROUP]
        c_block = mixed[rows, GROUP:]
        c_held[block] = c_block
        b_turned[block] = jnp.transpose(b_block.astype(F32)).astype(BF16)
        scores[block] = jnp.where(
            causal, jnp.dot(c_block, b_turned[block], preferred_element_type=F32), 0.0
        )
    def state_copy(chunk):
        return pltpu.make_async_remote_copy(
            src_ref=leaving_state.at[chunk],
            dst_ref=arriving_state.at[chunk],
            send_sem=state_send.at[chunk],
            recv_sem=state_recv.at[chunk],
            device_id=(dp, (seq + 1) % seq_count),
            device_id_type=MESH,
        )

    def out_columns(chunk):
        return pl.ds(pl.multiple_of(chunk * CHUNK, CHUNK), CHUNK)

    def work(chunk, carry):
        slab = chunk + 1

        whole_slab(slab)
        project(slab, pl.multiple_of(chunk * CHUNK, CHUNK))

        @pl.when(slab + 2 < slab_count)
        def _():
            pass_x(slab + 2)

        fadings = []
        for block in range(block_count):
            rows = slice(block * GROUP, (block + 1) * GROUP)
            decay = decay_held[chunk, :head_count, rows]
            across = across_held[chunk, :head_count, rows]
            down = down_held[chunk, rows, :head_count]
            closing = down[GROUP - 1 : GROUP, :]
            scale = jnp.exp(closing - down) * (-down_decay_held[chunk, rows, :head_count])
            fading = jnp.exp(closing)
            grown = jnp.exp(down)
            fades = []
            for pair in range(head_count // 2):
                lanes = slice(pair * GROUP, (pair + 1) * GROUP)
                x_pair = mixed[rows, lanes]
                x_wide = x_pair.astype(F32)
                weights = []
                for head in (2 * pair, 2 * pair + 1):
                    gap = down[:, head : head + 1] - across[head : head + 1, :]
                    weights.append(
                        (
                            scores[block]
                            * jnp.exp(jnp.minimum(gap, 0.0))
                            * (-decay[head : head + 1, :])
                        ).astype(BF16)
                    )
                x_apart = jnp.concatenate(
                    [jnp.where(first_head, x_wide, 0.0), jnp.where(first_head, 0.0, x_wide)], axis=0
                ).astype(BF16)
                skips = jnp.where(
                    first_head,
                    skip_ref[chunk * head_count + 2 * pair],
                    skip_ref[chunk * head_count + 2 * pair + 1],
                )
                intra[rows, lanes] = (
                    jnp.dot(
                        jnp.concatenate(weights, axis=1), x_apart, preferred_element_type=F32
                    )
                    + skips * x_wide
                )
                scaled = (both(scale, pair) * x_wide).astype(BF16)
                block_states[block, :, lanes] = jnp.dot(
                    b_turned[block], scaled, preferred_element_type=F32
                )
                expanded[rows, lanes] = both(grown, pair)
                fades.append(both(fading, pair))
            fadings.append(jnp.concatenate(fades, axis=1))

        @pl.when(slab + 1 < slab_count)
        def _():
            pass_core(slab + 1)

        @pl.when(seq > 0)
        def _():
            state_copy(chunk).wait_recv()

        @pl.when(seq == 0)
        def _():
            arriving_state[chunk] = jnp.zeros(arriving_state.shape[1:], F32)

        state = arriving_state[chunk]
        for block in range(block_count):
            entering_half[block] = state.astype(BF16)
            state = fadings[block] * state + block_states[block]
        leaving_state[chunk] = state

        @pl.when(seq < seq_count - 1)
        def _():
            state_copy(chunk).start()

        gains = out_gain_ref[:, out_columns(chunk)]
        for block in range(block_count):
            rows = slice(block * GROUP, (block + 1) * GROUP)
            inter = jnp.dot(c_held[block], entering_half[block], preferred_element_type=F32)
            ssm = intra[rows, :] + inter * expanded[rows, :]
            square = ssm * ssm
            high = square.astype(BF16)
            low = (square - high.astype(F32)).astype(BF16)
            for pair in range(head_count // 2):
                lanes = slice(pair * GROUP, (pair + 1) * GROUP)
                total = jnp.dot(
                    jnp.concatenate([high[:, lanes], low[:, lanes]], axis=1),
                    same_head_twice,
                    preferred_element_type=F32,
                )
                head_scale = lax.rsqrt(total * (1.0 / head_width) + 1e-05)
                normalized[rows, lanes] = (
                    ssm[:, lanes] * head_scale * gains[:, lanes]
                ).astype(BF16)
        picked[chunk] = jnp.dot(choice[...], normalized[...], preferred_element_type=F32).astype(BF16)
        for k in range(1, seq_count):
            target = (seq + k) % seq_count
            pltpu.make_async_remote_copy(
                src_ref=picked.at[chunk, pl.ds(pl.multiple_of(target * share, share), share)],
                dst_ref=result_ref.at[seq, :, out_columns(chunk)],
                send_sem=out_send.at[k - 1],
                recv_sem=out_recv.at[k - 1],
                device_id=(dp, target),
                device_id_type=MESH,
            ).start()
        pltpu.make_async_copy(
            picked.at[chunk, pl.ds(pl.multiple_of(seq * share, share), share)],
            result_ref.at[seq, :, out_columns(chunk)],
            own_sem,
        ).start()
        return carry

    lax.fori_loop(0, chunk_count, work, 0)

    for k in range(1, seq_count):
        source = (seq + seq_count - k) % seq_count
        whole = pltpu.make_async_remote_copy(
            src_ref=result_ref.at[source],
            dst_ref=result_ref.at[source],
            send_sem=out_send.at[k - 1],
            recv_sem=out_recv.at[k - 1],
            device_id=(dp, (seq + k) % seq_count),
            device_id_type=MESH,
        )
        whole.wait_recv()
        whole.wait_send()
    pltpu.make_async_copy(result_ref.at[seq], result_ref.at[seq], own_sem).wait()

    def settle(slab, carry):
        for k in range(1, z_count):
            z_copy(slab, k, z).wait_send()
        for k in range(1, x_count):
            x_copy(slab, k, x, slice(None)).wait_send()
        if core_count > 1:
            core_copy(slab, core).wait_send()
        return carry

    lax.fori_loop(0, slab_count, settle, 0)

    @pl.when(seq < seq_count - 1)
    def _():
        halo_copy.wait_send()

        def state_settle(chunk, carry):
            state_copy(chunk).wait_send()
            return carry

        lax.fori_loop(0, chunk_count, state_settle, 0)


def interleave_kernel(frame_count, arrived_ref, out_ref):
    share = arrived_ref.shape[1]
    step = min(share, max(GROUP // frame_count, 16))
    rows = step * frame_count
    row = lax.broadcasted_iota(jnp.int32, (rows, rows), 0)
    column = lax.broadcasted_iota(jnp.int32, (rows, rows), 1)
    frame = column // step
    choice = jnp.where(row == (column - frame * step) * frame_count + frame, 1.0, 0.0).astype(BF16)
    for first in range(0, share, step):
        block = jnp.concatenate(
            [arrived_ref[f, first : first + step, :] for f in range(frame_count)], axis=0
        )
        out_ref[first * frame_count : first * frame_count + rows, :] = jnp.dot(
            choice, block, preferred_element_type=F32
        ).astype(BF16)


def on_device(
    sizes, tokens, in_gain, in_weight, conv_weight, conv_bias, log_decay, skip, out_gain, scan_order
):
    z_count, x_count, core_count, seq_count = sizes
    token_count, width = tokens.shape[1:]
    own_rows, channels = in_weight.shape
    heads = log_decay.shape[1]
    inner = out_gain.shape[0]
    head_width = inner // heads
    chunk_count = inner // CHUNK
    slab_count = chunk_count + 1
    per_chunk = heads // chunk_count
    taps = conv_weight.shape[0]
    positions = scan_order.shape[0]
    share = positions // seq_count
    assert token_count == positions and channels == inner + 2 * GROUP and per_chunk == 4

    vmem = pl.BlockSpec(memory_space=pltpu.VMEM)
    smem = pl.BlockSpec(memory_space=pltpu.SMEM)
    hbm = pl.BlockSpec(memory_space=pl.ANY)
    block_count = token_count // GROUP
    hops = max(z_count - 1, 1), max(x_count - 1, 1), max(seq_count - 1, 1)
    arrived = pl.pallas_call(
        functools.partial(fused_kernel, sizes + (head_width,)),
        out_shape=jax.ShapeDtypeStruct((seq_count, share, inner), BF16),
        in_specs=[hbm, vmem, hbm, vmem, vmem, vmem, smem, vmem, vmem],
        out_specs=pl.BlockSpec(memory_space=pl.ANY),
        scratch_shapes=[
            pltpu.VMEM((token_count, width), BF16),
            pltpu.VMEM(
                (slab_count, z_count, x_count, core_count, own_rows // core_count, CHUNK), BF16
            ),
            pltpu.VMEM((HALO + token_count, width), BF16),
            pltpu.VMEM((positions, positions), BF16),
            pltpu.VMEM((chunk_count, token_count, GROUP), F32),
            pltpu.VMEM((chunk_count, token_count, GROUP), F32),
            pltpu.VMEM((chunk_count, 8, token_count), F32),
            pltpu.VMEM((chunk_count, 8, token_count), F32),
            pltpu.VMEM((HALO + token_count, CHUNK), F32),
            pltpu.VMEM((token_count, CHUNK), BF16),
            pltpu.VMEM((token_count // GROUP, GROUP, GROUP), BF16),
            pltpu.VMEM((token_count // GROUP, GROUP, GROUP), BF16),
            pltpu.VMEM((token_count // GROUP, GROUP, GROUP), F32),
            pltpu.VMEM((token_count // GROUP, GROUP, CHUNK), F32),
            pltpu.VMEM((token_count // GROUP, GROUP, CHUNK), BF16),
            pltpu.VMEM((token_count, CHUNK), F32),
            pltpu.VMEM((token_count, CHUNK), F32),
            pltpu.VMEM((chunk_count, GROUP, CHUNK), F32),
            pltpu.VMEM((chunk_count, GROUP, CHUNK), F32),
            pltpu.VMEM((token_count, CHUNK), BF16),
            pltpu.VMEM((chunk_count, positions, CHUNK), BF16),
            pltpu.SemaphoreType.DMA((slab_count, hops[0])),
            pltpu.SemaphoreType.DMA((slab_count, hops[0])),
            pltpu.SemaphoreType.DMA((slab_count, hops[1])),
            pltpu.SemaphoreType.DMA((slab_count, hops[1])),
            pltpu.SemaphoreType.DMA((slab_count,)),
            pltpu.SemaphoreType.DMA((slab_count,)),
            pltpu.SemaphoreType.DMA,
            pltpu.SemaphoreType.DMA,
            pltpu.SemaphoreType.DMA((chunk_count,)),
            pltpu.SemaphoreType.DMA((chunk_count,)),
            pltpu.SemaphoreType.DMA((hops[2],)),
            pltpu.SemaphoreType.DMA((hops[2],)),
            pltpu.SemaphoreType.DMA,
            pltpu.SemaphoreType.DMA((block_count,)),
            pltpu.SemaphoreType.DMA((slab_count,)),
        ],
        compiler_params=pltpu.CompilerParams(
            collective_id=0, has_side_effects=True, vmem_limit_bytes=52 * 1024 * 1024
        ),
        name="projected_scan",
    )(
        tokens[0],
        in_gain.reshape(1, width),
        in_weight,
        conv_weight,
        conv_bias.reshape(1, channels),
        log_decay[0],
        skip,
        out_gain.reshape(1, inner),
        scan_order.reshape(1, positions),
    )
    columns = min(512, inner)
    out = pl.pallas_call(
        functools.partial(interleave_kernel, seq_count),
        out_shape=jax.ShapeDtypeStruct((token_count, inner), BF16),
        grid=(inner // columns,),
        in_specs=[pl.BlockSpec((seq_count, share, columns), lambda i: (0, 0, i))],
        out_specs=pl.BlockSpec((token_count, columns), lambda i: (0, i)),
        name="frames_within_positions",
    )(arrived)
    return out[None]


def solution(mesh):
    dp_count, seq_count = mesh.shape["dp"], mesh.shape["seq"]
    x_count = 2 ** (int(math.log2(dp_count)) // 2)
    while dp_count % x_count:
        x_count //= 2
    sizes = (dp_count // x_count, x_count, 2 if seq_count % 2 == 0 else 1, seq_count)
    in_specs = (
        P("dp", "seq", None),
        P(),
        P("dp", None),
        P(),
        P(),
        P("dp", None, "seq"),
        P(),
        P(),
        P(),
    )
    return jax.shard_map(
        functools.partial(on_device, sizes),
        mesh=mesh,
        in_specs=in_specs,
        out_specs=P("dp", "seq", None),
        check_vma=False,
    )
```

```python
import functools
import math

import jax
import jax.numpy as jnp
from jax import lax
from jax.experimental import pallas as pl
from jax.experimental.pallas import tpu as pltpu
from jax.sharding import PartitionSpec as P

GROUP = 128
CHUNK = 256
HALO = 16
WINDOW = 3
BF16 = jnp.bfloat16
F32 = jnp.float32
MESH = pl.DeviceIdType.MESH


def fused_kernel(
    sizes,
    tokens_hbm,
    gain_hbm,
    weight_hbm,
    conv_weight_hbm,
    conv_bias_hbm,
    decay_hbm,
    skip_hbm,
    out_gain_hbm,
    order_hbm,
    result_ref,
    tokens_ref,
    gain_ref,
    conv_weight_ref,
    conv_bias_ref,
    decay_ref,
    skip_ref,
    out_gain_ref,
    order_ref,
    skip_held,
    bias_held,
    arrived,
    together,
    slabs,
    normed,
    choice,
    down_held,
    down_decay_held,
    across_held,
    decay_held,
    projected,
    mixed,
    b_turned,
    c_held,
    scores,
    block_states,
    entering_half,
    intra,
    expanded,
    arriving_state,
    leaving_state,
    normalized,
    picked,
    z_send,
    z_recv,
    x_send,
    x_recv,
    core_send,
    core_recv,
    halo_send,
    halo_recv,
    state_send,
    state_recv,
    out_send,
    out_recv,
    own_sem,
    token_sem,
    weight_sem,
    small_sem,
):
    z_count, x_count, core_count, seq_count, head_width = sizes
    head_count = CHUNK // head_width
    dp = lax.axis_index("dp")
    seq = lax.axis_index("seq")
    z = dp // x_count
    x = dp % x_count
    core = seq % core_count
    sibling = seq - core + (core + 1) % core_count
    half = slabs.shape[4]
    slab_count = slabs.shape[0]
    chunk_count = slab_count - 1
    token_count, width = tokens_ref.shape
    block_count = token_count // GROUP
    positions = order_ref.shape[1]
    share = positions // seq_count

    partners = [(((z + k) % z_count) * x_count + x, seq) for k in range(1, z_count)]
    partners += [(z * x_count + (x + k) % x_count, seq) for k in range(1, x_count)]
    partners += [(dp, (seq + k) % seq_count) for k in range(1, seq_count)]
    barrier = pltpu.get_barrier_semaphore()
    for partner in partners:
        pl.semaphore_signal(barrier, inc=1, device_id=partner, device_id_type=MESH)

    own_rows = pl.ds(pl.multiple_of(core * half, half), half)

    def load_weight(slab):
        first = chunk_count * CHUNK if slab == 0 else (slab - 1) * CHUNK
        return pltpu.make_async_copy(
            weight_hbm.at[own_rows, first : first + CHUNK],
            slabs.at[slab, z, x, core],
            weight_sem.at[slab],
        )

    def load_tokens(block):
        rows = slice(block * GROUP, (block + 1) * GROUP)
        return pltpu.make_async_copy(tokens_hbm.at[rows], tokens_ref.at[rows], token_sem.at[block])

    small = [
        pltpu.make_async_copy(source, target, small_sem.at[i])
        for i, (source, target) in enumerate(
            [
                (gain_hbm, gain_ref),
                (conv_weight_hbm, conv_weight_ref),
                (conv_bias_hbm, conv_bias_ref),
                (decay_hbm, decay_ref),
                (skip_hbm, skip_ref),
                (out_gain_hbm, out_gain_ref),
                (order_hbm, order_ref),
            ]
        )
    ]
    for slab in range(slab_count):
        load_weight(slab).start()
    for block in range(block_count):
        load_tokens(block).start()
    for copy in small:
        copy.start()
    for slab in range(slab_count):
        load_weight(slab).wait()
    pl.semaphore_wait(barrier, len(partners))

    def z_copy(slab, k, source):
        return pltpu.make_async_remote_copy(
            src_ref=slabs.at[slab, source, x, core],
            dst_ref=slabs.at[slab, source, x, core],
            send_sem=z_send.at[slab, k - 1],
            recv_sem=z_recv.at[slab, k - 1],
            device_id=(((z + k) % z_count) * x_count + x, seq),
            device_id_type=MESH,
        )

    def x_copy(slab, k, source, row):
        piece = slabs.at[slab, row, source, core]
        return pltpu.make_async_remote_copy(
            src_ref=piece,
            dst_ref=piece,
            send_sem=x_send.at[slab, k - 1],
            recv_sem=x_recv.at[slab, k - 1],
            device_id=(z * x_count + (x + k) % x_count, seq),
            device_id_type=MESH,
        )

    def core_copy(slab, source):
        return pltpu.make_async_remote_copy(
            src_ref=slabs.at[slab, :, :, source],
            dst_ref=slabs.at[slab, :, :, source],
            send_sem=core_send.at[slab],
            recv_sem=core_recv.at[slab],
            device_id=(dp, sibling),
            device_id_type=MESH,
        )

    def send_own(slab):
        for k in range(1, z_count):
            z_copy(slab, k, z).start()
        for k in range(1, x_count):
            x_copy(slab, k, x, z).start()

    def pass_x(slab):
        for k in range(1, z_count):
            row = (z + z_count - k) % z_count
            z_copy(slab, k, row).wait_recv()
            for kx in range(1, x_count):
                x_copy(slab, kx, x, row).start()

        if isinstance(slab, int):
            if slab + WINDOW < slab_count:
                send_own(slab + WINDOW)
        else:

            @pl.when(slab + WINDOW < slab_count)
            def _():
                send_own(slab + WINDOW)

    def pass_core(slab):
        for k in range(1, x_count):
            x_copy(slab, k, (x + x_count - k) % x_count, slice(None)).wait_recv()
        if core_count > 1:
            core_copy(slab, core).start()

    def whole_slab(slab):
        if core_count > 1:
            core_copy(slab, (core + 1) % core_count).wait_recv()

    for slab in range(min(WINDOW, slab_count)):
        send_own(slab)

    for copy in small:
        copy.wait()
    for block in range(block_count):
        load_tokens(block).wait()
        rows = tokens_ref[block * GROUP : (block + 1) * GROUP, :].astype(F32)
        inverse = lax.rsqrt(jnp.mean(rows * rows, axis=1, keepdims=True) + 1e-05)
        normed[HALO + block * GROUP : HALO + (block + 1) * GROUP, :] = (
            rows * inverse * gain_ref[...]
        ).astype(BF16)

    halo_copy = pltpu.make_async_remote_copy(
        src_ref=normed.at[token_count : token_count + HALO],
        dst_ref=normed.at[0:HALO],
        send_sem=halo_send,
        recv_sem=halo_recv,
        device_id=(dp, (seq + 1) % seq_count),
        device_id_type=MESH,
    )

    @pl.when(seq < seq_count - 1)
    def _():
        halo_copy.start()

    @pl.when(seq == 0)
    def _():
        normed[0:HALO, :] = jnp.zeros((HALO, width), BF16)

    row_at = lax.broadcasted_iota(jnp.int32, (GROUP, GROUP), 0)
    column_at = lax.broadcasted_iota(jnp.int32, (GROUP, GROUP), 1)
    causal = column_at <= row_at
    lower = jnp.where(causal, 1.0, 0.0).astype(F32)
    unit = jnp.where(row_at == column_at, 1.0, 0.0).astype(F32)
    upper = jnp.where(row_at <= column_at, 1.0, 0.0).astype(F32)
    first_head = lax.broadcasted_iota(jnp.int32, (1, GROUP), 1) < head_width
    same_head = jnp.where(row_at // head_width == column_at // head_width, 1.0, 0.0).astype(BF16)
    same_head_twice = jnp.concatenate([same_head, same_head], axis=0)

    def project(slab, first_column):
        columns = pl.ds(first_column, CHUNK)
        matrix = slabs[slab].reshape(width, CHUNK)
        projected[...] = (
            jnp.dot(normed[...], matrix, preferred_element_type=F32).astype(BF16).astype(F32)
        )
        taps = conv_weight_ref.shape[0]
        for block in range(block_count):
            total = bias_held[slab]
            for tap in range(taps):
                first = HALO + block * GROUP + tap - (taps - 1)
                total = total + conv_weight_ref[tap : tap + 1, columns] * projected[
                    first : first + GROUP, :
                ]
            mixed[block * GROUP : (block + 1) * GROUP, :] = (
                0.5 * total * (1.0 + jnp.tanh(0.5 * total))
            ).astype(BF16)

    def both(columns, pair):
        return jnp.where(
            first_head, columns[:, 2 * pair : 2 * pair + 1], columns[:, 2 * pair + 1 : 2 * pair + 2]
        )

    pass_x(0)
    for slab in range(slab_count):
        first = chunk_count * CHUNK if slab == 0 else (slab - 1) * CHUNK
        bias_held[slab] = conv_bias_ref[first : first + CHUNK].reshape(1, CHUNK)
    for chunk in range(chunk_count):
        for pair in range(head_count // 2):
            head = chunk * head_count + 2 * pair
            skip_held[chunk, :, pair * GROUP : (pair + 1) * GROUP] = jnp.where(
                first_head, skip_ref[:, head : head + 1], skip_ref[:, head + 1 : head + 2]
            )
    for block in range(block_count):
        rows = slice(block * GROUP, (block + 1) * GROUP)
        decay = decay_ref[:, rows]
        across = jnp.dot(decay, upper, precision=lax.Precision.HIGHEST, preferred_element_type=F32)
        turned = (((1,), (1,)), ((), ()))
        down = lax.dot_general(
            lower, decay, turned, precision=lax.Precision.HIGHEST, preferred_element_type=F32
        )
        down_decay = lax.dot_general(
            unit, decay, turned, precision=lax.Precision.HIGHEST, preferred_element_type=F32
        )
        for chunk in range(chunk_count):
            heads = slice(chunk * head_count, (chunk + 1) * head_count)
            down_held[chunk, rows, :head_count] = down[:, heads]
            down_decay_held[chunk, rows, :head_count] = down_decay[:, heads]
            across_held[chunk, :head_count, rows] = across[heads, :]
            decay_held[chunk, :head_count, rows] = decay[heads, :]
    pass_core(0)
    pass_x(1)
    choice[...] = jnp.transpose(
        jnp.where(
            lax.broadcasted_iota(jnp.int32, (positions, positions), 0) == order_ref[...], 1.0, 0.0
        ).astype(F32)
    ).astype(BF16)

    @pl.when(seq > 0)
    def _():
        halo_copy.wait_recv()

    whole_slab(0)
    project(0, chunk_count * CHUNK)
    pass_x(2)
    pass_core(1)
    for block in range(block_count):
        rows = slice(block * GROUP, (block + 1) * GROUP)
        b_block = mixed[rows, :GROUP]
        c_block = mixed[rows, GROUP:]
        c_held[block] = c_block
        b_turned[block] = jnp.transpose(b_block.astype(F32)).astype(BF16)
        scores[block] = jnp.where(
            causal, jnp.dot(c_block, b_turned[block], preferred_element_type=F32), 0.0
        )
    def state_copy(chunk):
        return pltpu.make_async_remote_copy(
            src_ref=leaving_state.at[chunk],
            dst_ref=arriving_state.at[chunk],
            send_sem=state_send.at[chunk],
            recv_sem=state_recv.at[chunk],
            device_id=(dp, (seq + 1) % seq_count),
            device_id_type=MESH,
        )

    def out_columns(chunk):
        return pl.ds(pl.multiple_of(chunk * CHUNK, CHUNK), CHUNK)

    def out_copy(chunk, k, source):
        target = (seq + k) % seq_count
        return pltpu.make_async_remote_copy(
            src_ref=picked.at[chunk, pl.ds(pl.multiple_of(target * share, share), share)],
            dst_ref=arrived.at[chunk, source],
            send_sem=out_send.at[chunk, k - 1],
            recv_sem=out_recv.at[chunk, k - 1],
            device_id=(dp, target),
            device_id_type=MESH,
        )

    step = min(share, max(GROUP // seq_count, 16))
    mixed_rows = step * seq_count
    row = lax.broadcasted_iota(jnp.int32, (mixed_rows, mixed_rows), 0)
    column = lax.broadcasted_iota(jnp.int32, (mixed_rows, mixed_rows), 1)
    frame = column // step
    frames_within = jnp.where(
        row == (column - frame * step) * seq_count + frame, 1.0, 0.0
    ).astype(BF16)

    def finish(chunk):
        for k in range(1, seq_count):
            out_copy(chunk, k, (seq + seq_count - k) % seq_count).wait_recv()
        for first in range(0, share, step):
            block = jnp.concatenate(
                [arrived[chunk, f, first : first + step, :] for f in range(seq_count)], axis=0
            )
            together[chunk, first * seq_count : first * seq_count + mixed_rows, :] = jnp.dot(
                frames_within, block, preferred_element_type=F32
            ).astype(BF16)
        pltpu.make_async_copy(
            together.at[chunk], result_ref.at[:, out_columns(chunk)], own_sem.at[chunk]
        ).start()

    def work(chunk, carry):
        slab = chunk + 1

        whole_slab(slab)
        project(slab, pl.multiple_of(chunk * CHUNK, CHUNK))

        @pl.when(slab + 2 < slab_count)
        def _():
            pass_x(slab + 2)

        fadings = []
        for block in range(block_count):
            rows = slice(block * GROUP, (block + 1) * GROUP)
            decay = decay_held[chunk, :head_count, rows]
            across = across_held[chunk, :head_count, rows]
            down = down_held[chunk, rows, :head_count]
            closing = down[GROUP - 1 : GROUP, :]
            scale = jnp.exp(closing - down) * (-down_decay_held[chunk, rows, :head_count])
            fading = jnp.exp(closing)
            grown = jnp.exp(down)
            fades = []
            for pair in range(head_count // 2):
                lanes = slice(pair * GROUP, (pair + 1) * GROUP)
                x_pair = mixed[rows, lanes]
                x_wide = x_pair.astype(F32)
                weights = []
                for head in (2 * pair, 2 * pair + 1):
                    gap = down[:, head : head + 1] - across[head : head + 1, :]
                    weights.append(
                        (
                            scores[block]
                            * jnp.exp(jnp.minimum(gap, 0.0))
                            * (-decay[head : head + 1, :])
                        ).astype(BF16)
                    )
                x_apart = jnp.concatenate(
                    [jnp.where(first_head, x_wide, 0.0), jnp.where(first_head, 0.0, x_wide)], axis=0
                ).astype(BF16)
                intra[rows, lanes] = (
                    jnp.dot(
                        jnp.concatenate(weights, axis=1), x_apart, preferred_element_type=F32
                    )
                    + skip_held[chunk, :, lanes] * x_wide
                )
                scaled = (both(scale, pair) * x_wide).astype(BF16)
                block_states[block, :, lanes] = jnp.dot(
                    b_turned[block], scaled, preferred_element_type=F32
                )
                expanded[rows, lanes] = both(grown, pair)
                fades.append(both(fading, pair))
            fadings.append(jnp.concatenate(fades, axis=1))

        @pl.when(slab + 1 < slab_count)
        def _():
            pass_core(slab + 1)

        @pl.when(chunk > 0)
        def _():
            finish(chunk - 1)

        @pl.when(seq > 0)
        def _():
            state_copy(chunk).wait_recv()

        @pl.when(seq == 0)
        def _():
            arriving_state[chunk] = jnp.zeros(arriving_state.shape[1:], F32)

        state = arriving_state[chunk]
        for block in range(block_count):
            entering_half[block] = state.astype(BF16)
            state = fadings[block] * state + block_states[block]
        leaving_state[chunk] = state

        @pl.when(seq < seq_count - 1)
        def _():
            state_copy(chunk).start()

        gains = out_gain_ref[:, out_columns(chunk)]
        for block in range(block_count):
            rows = slice(block * GROUP, (block + 1) * GROUP)
            inter = jnp.dot(c_held[block], entering_half[block], preferred_element_type=F32)
            ssm = intra[rows, :] + inter * expanded[rows, :]
            square = ssm * ssm
            high = square.astype(BF16)
            low = (square - high.astype(F32)).astype(BF16)
            for pair in range(head_count // 2):
                lanes = slice(pair * GROUP, (pair + 1) * GROUP)
                total = jnp.dot(
                    jnp.concatenate([high[:, lanes], low[:, lanes]], axis=1),
                    same_head_twice,
                    preferred_element_type=F32,
                )
                head_scale = lax.rsqrt(total * (1.0 / head_width) + 1e-05)
                normalized[rows, lanes] = (
                    ssm[:, lanes] * head_scale * gains[:, lanes]
                ).astype(BF16)
        picked[chunk] = jnp.dot(choice[...], normalized[...], preferred_element_type=F32).astype(BF16)
        for k in range(1, seq_count):
            out_copy(chunk, k, seq).start()
        arrived[chunk, seq] = picked[chunk, pl.ds(pl.multiple_of(seq * share, share), share)]
        return carry

    lax.fori_loop(0, chunk_count, work, 0)

    finish(chunk_count - 1)

    def out_settle(chunk, carry):
        for k in range(1, seq_count):
            out_copy(chunk, k, seq).wait_send()
        pltpu.make_async_copy(
            together.at[chunk], result_ref.at[:, out_columns(chunk)], own_sem.at[chunk]
        ).wait()
        return carry

    lax.fori_loop(0, chunk_count, out_settle, 0)

    def settle(slab, carry):
        for k in range(1, z_count):
            z_copy(slab, k, z).wait_send()
        for k in range(1, x_count):
            x_copy(slab, k, x, slice(None)).wait_send()
        if core_count > 1:
            core_copy(slab, core).wait_send()
        return carry

    lax.fori_loop(0, slab_count, settle, 0)

    @pl.when(seq < seq_count - 1)
    def _():
        halo_copy.wait_send()

        def state_settle(chunk, carry):
            state_copy(chunk).wait_send()
            return carry

        lax.fori_loop(0, chunk_count, state_settle, 0)


def on_device(
    sizes, tokens, in_gain, in_weight, conv_weight, conv_bias, log_decay, skip, out_gain, scan_order
):
    z_count, x_count, core_count, seq_count = sizes
    token_count, width = tokens.shape[1:]
    own_rows, channels = in_weight.shape
    heads = log_decay.shape[1]
    inner = out_gain.shape[0]
    head_width = inner // heads
    chunk_count = inner // CHUNK
    slab_count = chunk_count + 1
    per_chunk = heads // chunk_count
    taps = conv_weight.shape[0]
    positions = scan_order.shape[0]
    share = positions // seq_count
    assert token_count == positions and channels == inner + 2 * GROUP and per_chunk == 4

    block_count = token_count // GROUP
    hops = max(z_count - 1, 1), max(x_count - 1, 1), max(seq_count - 1, 1)
    regrouped = pl.pallas_call(
        functools.partial(fused_kernel, sizes + (head_width,)),
        out_shape=jax.ShapeDtypeStruct((token_count, inner), BF16),
        in_specs=[pl.BlockSpec(memory_space=pl.ANY)] * 9,
        out_specs=pl.BlockSpec(memory_space=pl.ANY),
        scratch_shapes=[
            pltpu.VMEM((token_count, width), BF16),
            pltpu.VMEM((1, width), F32),
            pltpu.VMEM((taps, channels), F32),
            pltpu.VMEM((channels,), F32),
            pltpu.VMEM((heads, token_count), F32),
            pltpu.VMEM((1, heads), F32),
            pltpu.VMEM((1, inner), F32),
            pltpu.VMEM((1, positions), jnp.int32),
            pltpu.VMEM((chunk_count, 1, CHUNK), F32),
            pltpu.VMEM((slab_count, 1, CHUNK), F32),
            pltpu.VMEM((chunk_count, seq_count, share, CHUNK), BF16),
            pltpu.VMEM((chunk_count, positions, CHUNK), BF16),
            pltpu.VMEM(
                (slab_count, z_count, x_count, core_count, own_rows // core_count, CHUNK), BF16
            ),
            pltpu.VMEM((HALO + token_count, width), BF16),
            pltpu.VMEM((positions, positions), BF16),
            pltpu.VMEM((chunk_count, token_count, GROUP), F32),
            pltpu.VMEM((chunk_count, token_count, GROUP), F32),
            pltpu.VMEM((chunk_count, 8, token_count), F32),
            pltpu.VMEM((chunk_count, 8, token_count), F32),
            pltpu.VMEM((HALO + token_count, CHUNK), F32),
            pltpu.VMEM((token_count, CHUNK), BF16),
            pltpu.VMEM((token_count // GROUP, GROUP, GROUP), BF16),
            pltpu.VMEM((token_count // GROUP, GROUP, GROUP), BF16),
            pltpu.VMEM((token_count // GROUP, GROUP, GROUP), F32),
            pltpu.VMEM((token_count // GROUP, GROUP, CHUNK), F32),
            pltpu.VMEM((token_count // GROUP, GROUP, CHUNK), BF16),
            pltpu.VMEM((token_count, CHUNK), F32),
            pltpu.VMEM((token_count, CHUNK), F32),
            pltpu.VMEM((chunk_count, GROUP, CHUNK), F32),
            pltpu.VMEM((chunk_count, GROUP, CHUNK), F32),
            pltpu.VMEM((token_count, CHUNK), BF16),
            pltpu.VMEM((chunk_count, positions, CHUNK), BF16),
            pltpu.SemaphoreType.DMA((slab_count, hops[0])),
            pltpu.SemaphoreType.DMA((slab_count, hops[0])),
            pltpu.SemaphoreType.DMA((slab_count, hops[1])),
            pltpu.SemaphoreType.DMA((slab_count, hops[1])),
            pltpu.SemaphoreType.DMA((slab_count,)),
            pltpu.SemaphoreType.DMA((slab_count,)),
            pltpu.SemaphoreType.DMA,
            pltpu.SemaphoreType.DMA,
            pltpu.SemaphoreType.DMA((chunk_count,)),
            pltpu.SemaphoreType.DMA((chunk_count,)),
            pltpu.SemaphoreType.DMA((chunk_count, hops[2])),
            pltpu.SemaphoreType.DMA((chunk_count, hops[2])),
            pltpu.SemaphoreType.DMA((chunk_count,)),
            pltpu.SemaphoreType.DMA((block_count,)),
            pltpu.SemaphoreType.DMA((slab_count,)),
            pltpu.SemaphoreType.DMA((7,)),
        ],
        compiler_params=pltpu.CompilerParams(
            collective_id=0, has_side_effects=True, vmem_limit_bytes=58 * 1024 * 1024
        ),
        name="projected_scan",
    )(
        tokens[0],
        in_gain.reshape(1, width),
        in_weight,
        conv_weight,
        conv_bias,
        log_decay[0],
        skip.reshape(1, heads),
        out_gain.reshape(1, inner),
        scan_order.reshape(1, positions),
    )
    return regrouped[None]


def solution(mesh):
    dp_count, seq_count = mesh.shape["dp"], mesh.shape["seq"]
    x_count = 2 ** (int(math.log2(dp_count)) // 2)
    while dp_count % x_count:
        x_count //= 2
    sizes = (dp_count // x_count, x_count, 2 if seq_count % 2 == 0 else 1, seq_count)
    in_specs = (
        P("dp", "seq", None),
        P(),
        P("dp", None),
        P(),
        P(),
        P("dp", None, "seq"),
        P(),
        P(),
        P(),
    )
    return jax.shard_map(
        functools.partial(on_device, sizes),
        mesh=mesh,
        in_specs=in_specs,
        out_specs=P("dp", "seq", None),
        check_vma=False,
    )
```

```python
import functools
import math

import jax
import jax.numpy as jnp
from jax import lax
from jax.experimental import pallas as pl
from jax.experimental.pallas import tpu as pltpu
from jax.sharding import PartitionSpec as P

GROUP = 128
CHUNK = 256
HALO = 16
WINDOW = 3
LAG = 2
BF16 = jnp.bfloat16
F32 = jnp.float32
MESH = pl.DeviceIdType.MESH


def fused_kernel(
    sizes,
    tokens_hbm,
    gain_hbm,
    weight_hbm,
    conv_weight_hbm,
    conv_bias_hbm,
    decay_hbm,
    skip_hbm,
    out_gain_hbm,
    order_hbm,
    result_ref,
    tokens_ref,
    gain_ref,
    conv_weight_ref,
    conv_bias_ref,
    decay_ref,
    skip_ref,
    out_gain_ref,
    order_ref,
    skip_held,
    bias_held,
    arrived,
    together,
    slabs,
    normed,
    choice,
    down_held,
    down_decay_held,
    across_held,
    decay_held,
    projected,
    mixed,
    b_turned,
    c_held,
    scores,
    block_states,
    entering_half,
    intra,
    expanded,
    arriving_state,
    leaving_state,
    normalized,
    picked,
    z_send,
    z_recv,
    x_send,
    x_recv,
    core_send,
    core_recv,
    halo_send,
    halo_recv,
    state_send,
    state_recv,
    out_send,
    out_recv,
    own_sem,
    token_sem,
    weight_sem,
    small_sem,
):
    z_count, x_count, core_count, seq_count, head_width = sizes
    head_count = CHUNK // head_width
    dp = lax.axis_index("dp")
    seq = lax.axis_index("seq")
    z = dp // x_count
    x = dp % x_count
    core = seq % core_count
    sibling = seq - core + (core + 1) % core_count
    half = slabs.shape[4]
    slab_count = slabs.shape[0]
    chunk_count = slab_count - 1
    token_count, width = tokens_ref.shape
    block_count = token_count // GROUP
    positions = order_ref.shape[1]
    share = positions // seq_count

    partners = [(((z + k) % z_count) * x_count + x, seq) for k in range(1, z_count)]
    partners += [(z * x_count + (x + k) % x_count, seq) for k in range(1, x_count)]
    partners += [(dp, (seq + k) % seq_count) for k in range(1, seq_count)]
    barrier = pltpu.get_barrier_semaphore()
    for partner in partners:
        pl.semaphore_signal(barrier, inc=1, device_id=partner, device_id_type=MESH)

    own_rows = pl.ds(pl.multiple_of(core * half, half), half)

    def load_weight(slab):
        first = chunk_count * CHUNK if slab == 0 else (slab - 1) * CHUNK
        return pltpu.make_async_copy(
            weight_hbm.at[own_rows, first : first + CHUNK],
            slabs.at[slab, z, x, core],
            weight_sem.at[slab],
        )

    def load_tokens(block):
        rows = slice(block * GROUP, (block + 1) * GROUP)
        return pltpu.make_async_copy(tokens_hbm.at[rows], tokens_ref.at[rows], token_sem.at[block])

    small = [
        pltpu.make_async_copy(source, target, small_sem.at[i])
        for i, (source, target) in enumerate(
            [
                (gain_hbm, gain_ref),
                (conv_weight_hbm, conv_weight_ref),
                (conv_bias_hbm, conv_bias_ref),
                (decay_hbm, decay_ref),
                (skip_hbm, skip_ref),
                (out_gain_hbm, out_gain_ref),
                (order_hbm, order_ref),
            ]
        )
    ]
    for slab in range(slab_count):
        load_weight(slab).start()
    for block in range(block_count):
        load_tokens(block).start()
    for copy in small:
        copy.start()
    for slab in range(slab_count):
        load_weight(slab).wait()
    pl.semaphore_wait(barrier, len(partners))

    def z_copy(slab, k, source):
        return pltpu.make_async_remote_copy(
            src_ref=slabs.at[slab, source, x, core],
            dst_ref=slabs.at[slab, source, x, core],
            send_sem=z_send.at[slab, k - 1],
            recv_sem=z_recv.at[slab, k - 1],
            device_id=(((z + k) % z_count) * x_count + x, seq),
            device_id_type=MESH,
        )

    def x_copy(slab, k, source, row):
        piece = slabs.at[slab, row, source, core]
        return pltpu.make_async_remote_copy(
            src_ref=piece,
            dst_ref=piece,
            send_sem=x_send.at[slab, k - 1],
            recv_sem=x_recv.at[slab, k - 1],
            device_id=(z * x_count + (x + k) % x_count, seq),
            device_id_type=MESH,
        )

    def core_copy(slab, source):
        return pltpu.make_async_remote_copy(
            src_ref=slabs.at[slab, :, :, source],
            dst_ref=slabs.at[slab, :, :, source],
            send_sem=core_send.at[slab],
            recv_sem=core_recv.at[slab],
            device_id=(dp, sibling),
            device_id_type=MESH,
        )

    def send_own(slab):
        for k in range(1, z_count):
            z_copy(slab, k, z).start()
        for k in range(1, x_count):
            x_copy(slab, k, x, z).start()

    def pass_x(slab):
        for k in range(1, z_count):
            row = (z + z_count - k) % z_count
            z_copy(slab, k, row).wait_recv()
            for kx in range(1, x_count):
                x_copy(slab, kx, x, row).start()

        if isinstance(slab, int):
            if slab + WINDOW < slab_count:
                send_own(slab + WINDOW)
        else:

            @pl.when(slab + WINDOW < slab_count)
            def _():
                send_own(slab + WINDOW)

    def pass_core(slab):
        for k in range(1, x_count):
            x_copy(slab, k, (x + x_count - k) % x_count, slice(None)).wait_recv()
        if core_count > 1:
            core_copy(slab, core).start()

    def whole_slab(slab):
        if core_count > 1:
            core_copy(slab, (core + 1) % core_count).wait_recv()

    for slab in range(min(WINDOW, slab_count)):
        send_own(slab)

    for copy in small:
        copy.wait()
    for block in range(block_count):
        load_tokens(block).wait()
        rows = tokens_ref[block * GROUP : (block + 1) * GROUP, :].astype(F32)
        inverse = lax.rsqrt(jnp.mean(rows * rows, axis=1, keepdims=True) + 1e-05)
        normed[HALO + block * GROUP : HALO + (block + 1) * GROUP, :] = (
            rows * inverse * gain_ref[...]
        ).astype(BF16)

    halo_copy = pltpu.make_async_remote_copy(
        src_ref=normed.at[token_count : token_count + HALO],
        dst_ref=normed.at[0:HALO],
        send_sem=halo_send,
        recv_sem=halo_recv,
        device_id=(dp, (seq + 1) % seq_count),
        device_id_type=MESH,
    )

    @pl.when(seq < seq_count - 1)
    def _():
        halo_copy.start()

    @pl.when(seq == 0)
    def _():
        normed[0:HALO, :] = jnp.zeros((HALO, width), BF16)

    row_at = lax.broadcasted_iota(jnp.int32, (GROUP, GROUP), 0)
    column_at = lax.broadcasted_iota(jnp.int32, (GROUP, GROUP), 1)
    causal = column_at <= row_at
    lower = jnp.where(causal, 1.0, 0.0).astype(F32)
    unit = jnp.where(row_at == column_at, 1.0, 0.0).astype(F32)
    upper = jnp.where(row_at <= column_at, 1.0, 0.0).astype(F32)
    first_head = lax.broadcasted_iota(jnp.int32, (1, GROUP), 1) < head_width
    same_head = jnp.where(row_at // head_width == column_at // head_width, 1.0, 0.0).astype(BF16)
    same_head_twice = jnp.concatenate([same_head, same_head], axis=0)

    def project(slab, first_column):
        columns = pl.ds(first_column, CHUNK)
        matrix = slabs[slab].reshape(width, CHUNK)
        projected[...] = (
            jnp.dot(normed[...], matrix, preferred_element_type=F32).astype(BF16).astype(F32)
        )
        taps = conv_weight_ref.shape[0]
        for block in range(block_count):
            total = bias_held[slab]
            for tap in range(taps):
                first = HALO + block * GROUP + tap - (taps - 1)
                total = total + conv_weight_ref[tap : tap + 1, columns] * projected[
                    first : first + GROUP, :
                ]
            mixed[block * GROUP : (block + 1) * GROUP, :] = (
                0.5 * total * (1.0 + jnp.tanh(0.5 * total))
            ).astype(BF16)

    def both(columns, pair):
        return jnp.where(
            first_head, columns[:, 2 * pair : 2 * pair + 1], columns[:, 2 * pair + 1 : 2 * pair + 2]
        )

    pass_x(0)
    for slab in range(slab_count):
        first = chunk_count * CHUNK if slab == 0 else (slab - 1) * CHUNK
        bias_held[slab] = conv_bias_ref[first : first + CHUNK].reshape(1, CHUNK)
    for chunk in range(chunk_count):
        for pair in range(head_count // 2):
            head = chunk * head_count + 2 * pair
            skip_held[chunk, :, pair * GROUP : (pair + 1) * GROUP] = jnp.where(
                first_head, skip_ref[:, head : head + 1], skip_ref[:, head + 1 : head + 2]
            )
    for block in range(block_count):
        rows = slice(block * GROUP, (block + 1) * GROUP)
        decay = decay_ref[:, rows]
        across = jnp.dot(decay, upper, precision=lax.Precision.HIGHEST, preferred_element_type=F32)
        turned = (((1,), (1,)), ((), ()))
        down = lax.dot_general(
            lower, decay, turned, precision=lax.Precision.HIGHEST, preferred_element_type=F32
        )
        down_decay = lax.dot_general(
            unit, decay, turned, precision=lax.Precision.HIGHEST, preferred_element_type=F32
        )
        for chunk in range(chunk_count):
            heads = slice(chunk * head_count, (chunk + 1) * head_count)
            down_held[chunk, rows, :head_count] = down[:, heads]
            down_decay_held[chunk, rows, :head_count] = down_decay[:, heads]
            across_held[chunk, :head_count, rows] = across[heads, :]
            decay_held[chunk, :head_count, rows] = decay[heads, :]
    pass_core(0)
    pass_x(1)
    choice[...] = jnp.transpose(
        jnp.where(
            lax.broadcasted_iota(jnp.int32, (positions, positions), 0) == order_ref[...], 1.0, 0.0
        ).astype(F32)
    ).astype(BF16)

    @pl.when(seq > 0)
    def _():
        halo_copy.wait_recv()

    whole_slab(0)
    project(0, chunk_count * CHUNK)
    pass_x(2)
    pass_core(1)
    for block in range(block_count):
        rows = slice(block * GROUP, (block + 1) * GROUP)
        b_block = mixed[rows, :GROUP]
        c_block = mixed[rows, GROUP:]
        c_held[block] = c_block
        b_turned[block] = jnp.transpose(b_block.astype(F32)).astype(BF16)
        scores[block] = jnp.where(
            causal, jnp.dot(c_block, b_turned[block], preferred_element_type=F32), 0.0
        )
    def state_copy(chunk):
        return pltpu.make_async_remote_copy(
            src_ref=leaving_state.at[chunk],
            dst_ref=arriving_state.at[chunk],
            send_sem=state_send.at[chunk],
            recv_sem=state_recv.at[chunk],
            device_id=(dp, (seq + 1) % seq_count),
            device_id_type=MESH,
        )

    def out_columns(chunk):
        return pl.ds(pl.multiple_of(chunk * CHUNK, CHUNK), CHUNK)

    def out_copy(chunk, k, source):
        target = (seq + k) % seq_count
        return pltpu.make_async_remote_copy(
            src_ref=picked.at[chunk, pl.ds(pl.multiple_of(target * share, share), share)],
            dst_ref=arrived.at[chunk, source],
            send_sem=out_send.at[chunk, k - 1],
            recv_sem=out_recv.at[chunk, k - 1],
            device_id=(dp, target),
            device_id_type=MESH,
        )

    step = min(share, max(GROUP // seq_count, 16))
    mixed_rows = step * seq_count
    row = lax.broadcasted_iota(jnp.int32, (mixed_rows, mixed_rows), 0)
    column = lax.broadcasted_iota(jnp.int32, (mixed_rows, mixed_rows), 1)
    frame = column // step
    frames_within = jnp.where(
        row == (column - frame * step) * seq_count + frame, 1.0, 0.0
    ).astype(BF16)

    def finish(chunk):
        for k in range(1, seq_count):
            out_copy(chunk, k, (seq + seq_count - k) % seq_count).wait_recv()
        for first in range(0, share, step):
            block = jnp.concatenate(
                [arrived[chunk, f, first : first + step, :] for f in range(seq_count)], axis=0
            )
            together[chunk, first * seq_count : first * seq_count + mixed_rows, :] = jnp.dot(
                frames_within, block, preferred_element_type=F32
            ).astype(BF16)
        pltpu.make_async_copy(
            together.at[chunk], result_ref.at[:, out_columns(chunk)], own_sem.at[chunk]
        ).start()

    def work(chunk, carry):
        slab = chunk + 1

        whole_slab(slab)
        project(slab, pl.multiple_of(chunk * CHUNK, CHUNK))

        @pl.when(slab + 2 < slab_count)
        def _():
            pass_x(slab + 2)

        fadings = []
        for block in range(block_count):
            rows = slice(block * GROUP, (block + 1) * GROUP)
            decay = decay_held[chunk, :head_count, rows]
            across = across_held[chunk, :head_count, rows]
            down = down_held[chunk, rows, :head_count]
            closing = down[GROUP - 1 : GROUP, :]
            scale = jnp.exp(closing - down) * (-down_decay_held[chunk, rows, :head_count])
            fading = jnp.exp(closing)
            grown = jnp.exp(down)
            fades = []
            for pair in range(head_count // 2):
                lanes = slice(pair * GROUP, (pair + 1) * GROUP)
                x_pair = mixed[rows, lanes]
                x_wide = x_pair.astype(F32)
                weights = []
                for head in (2 * pair, 2 * pair + 1):
                    gap = down[:, head : head + 1] - across[head : head + 1, :]
                    weights.append(
                        (
                            scores[block]
                            * jnp.exp(jnp.minimum(gap, 0.0))
                            * (-decay[head : head + 1, :])
                        ).astype(BF16)
                    )
                x_apart = jnp.concatenate(
                    [jnp.where(first_head, x_wide, 0.0), jnp.where(first_head, 0.0, x_wide)], axis=0
                ).astype(BF16)
                intra[rows, lanes] = (
                    jnp.dot(
                        jnp.concatenate(weights, axis=1), x_apart, preferred_element_type=F32
                    )
                    + skip_held[chunk, :, lanes] * x_wide
                )
                scaled = (both(scale, pair) * x_wide).astype(BF16)
                block_states[block, :, lanes] = jnp.dot(
                    b_turned[block], scaled, preferred_element_type=F32
                )
                expanded[rows, lanes] = both(grown, pair)
                fades.append(both(fading, pair))
            fadings.append(jnp.concatenate(fades, axis=1))

        @pl.when(slab + 1 < slab_count)
        def _():
            pass_core(slab + 1)

        @pl.when(seq > 0)
        def _():
            state_copy(chunk).wait_recv()

        @pl.when(seq == 0)
        def _():
            arriving_state[chunk] = jnp.zeros(arriving_state.shape[1:], F32)

        state = arriving_state[chunk]
        for block in range(block_count):
            entering_half[block] = state.astype(BF16)
            state = fadings[block] * state + block_states[block]
        leaving_state[chunk] = state

        @pl.when(seq < seq_count - 1)
        def _():
            state_copy(chunk).start()

        gains = out_gain_ref[:, out_columns(chunk)]
        for block in range(block_count):
            rows = slice(block * GROUP, (block + 1) * GROUP)
            inter = jnp.dot(c_held[block], entering_half[block], preferred_element_type=F32)
            ssm = intra[rows, :] + inter * expanded[rows, :]
            square = ssm * ssm
            high = square.astype(BF16)
            low = (square - high.astype(F32)).astype(BF16)
            for pair in range(head_count // 2):
                lanes = slice(pair * GROUP, (pair + 1) * GROUP)
                total = jnp.dot(
                    jnp.concatenate([high[:, lanes], low[:, lanes]], axis=1),
                    same_head_twice,
                    preferred_element_type=F32,
                )
                head_scale = lax.rsqrt(total * (1.0 / head_width) + 1e-05)
                normalized[rows, lanes] = (
                    ssm[:, lanes] * head_scale * gains[:, lanes]
                ).astype(BF16)
        picked[chunk] = jnp.dot(choice[...], normalized[...], preferred_element_type=F32).astype(BF16)
        for k in range(1, seq_count):
            out_copy(chunk, k, seq).start()
        arrived[chunk, seq] = picked[chunk, pl.ds(pl.multiple_of(seq * share, share), share)]

        @pl.when(chunk >= LAG)
        def _():
            finish(chunk - LAG)

        return carry

    lax.fori_loop(0, chunk_count, work, 0)

    for chunk in range(max(chunk_count - LAG, 0), chunk_count):
        finish(chunk)

    def out_settle(chunk, carry):
        for k in range(1, seq_count):
            out_copy(chunk, k, seq).wait_send()
        pltpu.make_async_copy(
            together.at[chunk], result_ref.at[:, out_columns(chunk)], own_sem.at[chunk]
        ).wait()
        return carry

    lax.fori_loop(0, chunk_count, out_settle, 0)

    def settle(slab, carry):
        for k in range(1, z_count):
            z_copy(slab, k, z).wait_send()
        for k in range(1, x_count):
            x_copy(slab, k, x, slice(None)).wait_send()
        if core_count > 1:
            core_copy(slab, core).wait_send()
        return carry

    lax.fori_loop(0, slab_count, settle, 0)

    @pl.when(seq < seq_count - 1)
    def _():
        halo_copy.wait_send()

        def state_settle(chunk, carry):
            state_copy(chunk).wait_send()
            return carry

        lax.fori_loop(0, chunk_count, state_settle, 0)


def on_device(
    sizes, tokens, in_gain, in_weight, conv_weight, conv_bias, log_decay, skip, out_gain, scan_order
):
    z_count, x_count, core_count, seq_count = sizes
    token_count, width = tokens.shape[1:]
    own_rows, channels = in_weight.shape
    heads = log_decay.shape[1]
    inner = out_gain.shape[0]
    head_width = inner // heads
    chunk_count = inner // CHUNK
    slab_count = chunk_count + 1
    per_chunk = heads // chunk_count
    taps = conv_weight.shape[0]
    positions = scan_order.shape[0]
    share = positions // seq_count
    assert token_count == positions and channels == inner + 2 * GROUP and per_chunk == 4

    block_count = token_count // GROUP
    hops = max(z_count - 1, 1), max(x_count - 1, 1), max(seq_count - 1, 1)
    regrouped = pl.pallas_call(
        functools.partial(fused_kernel, sizes + (head_width,)),
        out_shape=jax.ShapeDtypeStruct((token_count, inner), BF16),
        in_specs=[pl.BlockSpec(memory_space=pl.ANY)] * 9,
        out_specs=pl.BlockSpec(memory_space=pl.ANY),
        scratch_shapes=[
            pltpu.VMEM((token_count, width), BF16),
            pltpu.VMEM((1, width), F32),
            pltpu.VMEM((taps, channels), F32),
            pltpu.VMEM((channels,), F32),
            pltpu.VMEM((heads, token_count), F32),
            pltpu.VMEM((1, heads), F32),
            pltpu.VMEM((1, inner), F32),
            pltpu.VMEM((1, positions), jnp.int32),
            pltpu.VMEM((chunk_count, 1, CHUNK), F32),
            pltpu.VMEM((slab_count, 1, CHUNK), F32),
            pltpu.VMEM((chunk_count, seq_count, share, CHUNK), BF16),
            pltpu.VMEM((chunk_count, positions, CHUNK), BF16),
            pltpu.VMEM(
                (slab_count, z_count, x_count, core_count, own_rows // core_count, CHUNK), BF16
            ),
            pltpu.VMEM((HALO + token_count, width), BF16),
            pltpu.VMEM((positions, positions), BF16),
            pltpu.VMEM((chunk_count, token_count, GROUP), F32),
            pltpu.VMEM((chunk_count, token_count, GROUP), F32),
            pltpu.VMEM((chunk_count, 8, token_count), F32),
            pltpu.VMEM((chunk_count, 8, token_count), F32),
            pltpu.VMEM((HALO + token_count, CHUNK), F32),
            pltpu.VMEM((token_count, CHUNK), BF16),
            pltpu.VMEM((token_count // GROUP, GROUP, GROUP), BF16),
            pltpu.VMEM((token_count // GROUP, GROUP, GROUP), BF16),
            pltpu.VMEM((token_count // GROUP, GROUP, GROUP), F32),
            pltpu.VMEM((token_count // GROUP, GROUP, CHUNK), F32),
            pltpu.VMEM((token_count // GROUP, GROUP, CHUNK), BF16),
            pltpu.VMEM((token_count, CHUNK), F32),
            pltpu.VMEM((token_count, CHUNK), F32),
            pltpu.VMEM((chunk_count, GROUP, CHUNK), F32),
            pltpu.VMEM((chunk_count, GROUP, CHUNK), F32),
            pltpu.VMEM((token_count, CHUNK), BF16),
            pltpu.VMEM((chunk_count, positions, CHUNK), BF16),
            pltpu.SemaphoreType.DMA((slab_count, hops[0])),
            pltpu.SemaphoreType.DMA((slab_count, hops[0])),
            pltpu.SemaphoreType.DMA((slab_count, hops[1])),
            pltpu.SemaphoreType.DMA((slab_count, hops[1])),
            pltpu.SemaphoreType.DMA((slab_count,)),
            pltpu.SemaphoreType.DMA((slab_count,)),
            pltpu.SemaphoreType.DMA,
            pltpu.SemaphoreType.DMA,
            pltpu.SemaphoreType.DMA((chunk_count,)),
            pltpu.SemaphoreType.DMA((chunk_count,)),
            pltpu.SemaphoreType.DMA((chunk_count, hops[2])),
            pltpu.SemaphoreType.DMA((chunk_count, hops[2])),
            pltpu.SemaphoreType.DMA((chunk_count,)),
            pltpu.SemaphoreType.DMA((block_count,)),
            pltpu.SemaphoreType.DMA((slab_count,)),
            pltpu.SemaphoreType.DMA((7,)),
        ],
        compiler_params=pltpu.CompilerParams(
            collective_id=0, has_side_effects=True, vmem_limit_bytes=58 * 1024 * 1024
        ),
        name="projected_scan",
    )(
        tokens[0],
        in_gain.reshape(1, width),
        in_weight,
        conv_weight,
        conv_bias,
        log_decay[0],
        skip.reshape(1, heads),
        out_gain.reshape(1, inner),
        scan_order.reshape(1, positions),
    )
    return regrouped[None]


def solution(mesh):
    dp_count, seq_count = mesh.shape["dp"], mesh.shape["seq"]
    x_count = 2 ** (int(math.log2(dp_count)) // 2)
    while dp_count % x_count:
        x_count //= 2
    sizes = (dp_count // x_count, x_count, 2 if seq_count % 2 == 0 else 1, seq_count)
    in_specs = (
        P("dp", "seq", None),
        P(),
        P("dp", None),
        P(),
        P(),
        P("dp", None, "seq"),
        P(),
        P(),
        P(),
    )
    return jax.shard_map(
        functools.partial(on_device, sizes),
        mesh=mesh,
        in_specs=in_specs,
        out_specs=P("dp", "seq", None),
        check_vma=False,
    )
```

```python
import functools
import math

import jax
import jax.numpy as jnp
from jax import lax
from jax.experimental import pallas as pl
from jax.experimental.pallas import tpu as pltpu
from jax.sharding import PartitionSpec as P

GROUP = 128
CHUNK = 256
HALO = 16
WINDOW = 3
SPLIT = 3
LAG = 2
BF16 = jnp.bfloat16
F32 = jnp.float32
MESH = pl.DeviceIdType.MESH


def fused_kernel(
    sizes,
    tokens_hbm,
    gain_hbm,
    weight_hbm,
    conv_weight_hbm,
    conv_bias_hbm,
    decay_hbm,
    skip_hbm,
    out_gain_hbm,
    order_hbm,
    result_ref,
    tokens_ref,
    gain_ref,
    conv_weight_ref,
    conv_bias_ref,
    decay_ref,
    skip_ref,
    out_gain_ref,
    order_ref,
    skip_held,
    bias_held,
    arrived,
    together,
    slabs,
    normed,
    choice,
    down_held,
    down_decay_held,
    across_held,
    decay_held,
    projected,
    mixed,
    b_turned,
    c_held,
    scores,
    block_states,
    entering_half,
    intra,
    expanded,
    arriving_state,
    leaving_state,
    normalized,
    picked,
    z_send,
    z_recv,
    x_send,
    x_recv,
    y_send,
    y_recv,
    core_send,
    core_recv,
    halo_send,
    halo_recv,
    state_send,
    state_recv,
    out_send,
    out_recv,
    own_sem,
    token_sem,
    weight_sem,
    small_sem,
):
    z_count, x_count, core_count, seq_count, head_width = sizes
    head_count = CHUNK // head_width
    dp = lax.axis_index("dp")
    seq = lax.axis_index("seq")
    z = dp // x_count
    x = dp % x_count
    core = seq % core_count
    planes = slabs.shape[2]
    plane = seq // core_count % planes
    sibling = seq - core + (core + 1) % core_count
    half = slabs.shape[5]
    slab_count = slabs.shape[0]
    chunk_count = slab_count - 1
    token_count, width = tokens_ref.shape
    block_count = token_count // GROUP
    positions = order_ref.shape[1]
    share = positions // seq_count

    partners = [(((z + k) % z_count) * x_count + x, seq) for k in range(1, z_count)]
    partners += [(z * x_count + (x + k) % x_count, seq) for k in range(1, x_count)]
    partners += [(dp, (seq + k) % seq_count) for k in range(1, seq_count)]
    barrier = pltpu.get_barrier_semaphore()
    for partner in partners:
        pl.semaphore_signal(barrier, inc=1, device_id=partner, device_id_type=MESH)

    def is_split(slab):
        if planes == 1:
            return False
        if isinstance(slab, int):
            return slab > 0 and slab % SPLIT == 0
        return jnp.logical_and(slab > 0, slab % SPLIT == 0)

    def where_true(condition, act):
        if isinstance(condition, bool):
            if condition:
                act()
        else:
            pl.when(condition)(act)

    def where_carried(slab, row, act):
        split = is_split(slab)
        if split is False:
            act()
        else:
            pl.when(jnp.logical_or(jnp.logical_not(split), row % planes == plane))(act)

    own_rows = pl.ds(pl.multiple_of(core * half, half), half)

    def load_weight(slab):
        first = chunk_count * CHUNK if slab == 0 else (slab - 1) * CHUNK
        return pltpu.make_async_copy(
            weight_hbm.at[own_rows, first : first + CHUNK],
            slabs.at[slab, z // planes, z % planes, x, core],
            weight_sem.at[slab],
        )

    def load_tokens(block):
        rows = slice(block * GROUP, (block + 1) * GROUP)
        return pltpu.make_async_copy(tokens_hbm.at[rows], tokens_ref.at[rows], token_sem.at[block])

    small = [
        pltpu.make_async_copy(source, target, small_sem.at[i])
        for i, (source, target) in enumerate(
            [
                (gain_hbm, gain_ref),
                (conv_weight_hbm, conv_weight_ref),
                (conv_bias_hbm, conv_bias_ref),
                (decay_hbm, decay_ref),
                (skip_hbm, skip_ref),
                (out_gain_hbm, out_gain_ref),
                (order_hbm, order_ref),
            ]
        )
    ]
    for slab in range(slab_count):
        where_carried(slab, z, load_weight(slab).start)
    for block in range(block_count):
        load_tokens(block).start()
    for copy in small:
        copy.start()
    for slab in range(slab_count):
        where_carried(slab, z, load_weight(slab).wait)
    pl.semaphore_wait(barrier, len(partners))

    def z_copy(slab, k, source):
        return pltpu.make_async_remote_copy(
            src_ref=slabs.at[slab, source // planes, source % planes, x, core],
            dst_ref=slabs.at[slab, source // planes, source % planes, x, core],
            send_sem=z_send.at[slab, k - 1],
            recv_sem=z_recv.at[slab, k - 1],
            device_id=(((z + k) % z_count) * x_count + x, seq),
            device_id_type=MESH,
        )

    def x_copy(slab, k, source, row):
        if row is None:
            piece = slabs.at[slab, :, :, source, core]
        elif isinstance(row, str):
            piece = slabs.at[slab, :, plane, source, core]
        else:
            piece = slabs.at[slab, row // planes, row % planes, source, core]
        return pltpu.make_async_remote_copy(
            src_ref=piece,
            dst_ref=piece,
            send_sem=x_send.at[slab, k - 1],
            recv_sem=x_recv.at[slab, k - 1],
            device_id=(z * x_count + (x + k) % x_count, seq),
            device_id_type=MESH,
        )

    def core_copy(slab, source):
        return pltpu.make_async_remote_copy(
            src_ref=slabs.at[slab, :, :, :, source],
            dst_ref=slabs.at[slab, :, :, :, source],
            send_sem=core_send.at[slab],
            recv_sem=core_recv.at[slab],
            device_id=(dp, sibling),
            device_id_type=MESH,
        )

    def y_copy(slab, k, source):
        piece = slabs.at[slab, :, source, :, core]
        return pltpu.make_async_remote_copy(
            src_ref=piece,
            dst_ref=piece,
            send_sem=y_send.at[slab // SPLIT - 1, k - 1],
            recv_sem=y_recv.at[slab // SPLIT - 1, k - 1],
            device_id=(dp, (plane + k) % planes * core_count + core),
            device_id_type=MESH,
        )

    def where_split(slab, act, otherwise):
        split = is_split(slab)
        where_true(split, act)
        where_true(not split if isinstance(split, bool) else jnp.logical_not(split), otherwise)

    def send_own(slab):
        def act():
            for k in range(1, z_count):
                z_copy(slab, k, z).start()
            for k in range(1, x_count):
                x_copy(slab, k, x, z).start()

        where_carried(slab, z, act)

    def pass_x(slab):
        for k in range(1, z_count):
            row = (z + z_count - k) % z_count

            def act(k=k, row=row):
                z_copy(slab, k, row).wait_recv()
                for kx in range(1, x_count):
                    x_copy(slab, kx, x, row).start()

            where_carried(slab, row, act)

        if isinstance(slab, int):
            if slab + WINDOW < slab_count:
                send_own(slab + WINDOW)
        else:

            @pl.when(slab + WINDOW < slab_count)
            def _():
                send_own(slab + WINDOW)

    def x_arrived(slab, rows):
        for k in range(1, x_count):
            x_copy(slab, k, (x + x_count - k) % x_count, rows).wait_recv()

    def pass_y(slab):
        def act():
            x_arrived(slab, "plane")
            for k in range(1, planes):
                y_copy(slab, k, plane).start()

        where_true(is_split(slab), act)

    def pass_core(slab):
        def y_arrived():
            for k in range(1, planes):
                y_copy(slab, k, (plane + planes - k) % planes).wait_recv()

        where_split(slab, y_arrived, lambda: x_arrived(slab, None))
        if core_count > 1:
            core_copy(slab, core).start()

    def whole_slab(slab):
        if core_count > 1:
            core_copy(slab, (core + 1) % core_count).wait_recv()

    for slab in range(min(WINDOW, slab_count)):
        send_own(slab)

    for copy in small:
        copy.wait()
    for block in range(block_count):
        load_tokens(block).wait()
        rows = tokens_ref[block * GROUP : (block + 1) * GROUP, :].astype(F32)
        inverse = lax.rsqrt(jnp.mean(rows * rows, axis=1, keepdims=True) + 1e-05)
        normed[HALO + block * GROUP : HALO + (block + 1) * GROUP, :] = (
            rows * inverse * gain_ref[...]
        ).astype(BF16)

    halo_copy = pltpu.make_async_remote_copy(
        src_ref=normed.at[token_count : token_count + HALO],
        dst_ref=normed.at[0:HALO],
        send_sem=halo_send,
        recv_sem=halo_recv,
        device_id=(dp, (seq + 1) % seq_count),
        device_id_type=MESH,
    )

    @pl.when(seq < seq_count - 1)
    def _():
        halo_copy.start()

    @pl.when(seq == 0)
    def _():
        normed[0:HALO, :] = jnp.zeros((HALO, width), BF16)

    row_at = lax.broadcasted_iota(jnp.int32, (GROUP, GROUP), 0)
    column_at = lax.broadcasted_iota(jnp.int32, (GROUP, GROUP), 1)
    causal = column_at <= row_at
    lower = jnp.where(causal, 1.0, 0.0).astype(F32)
    unit = jnp.where(row_at == column_at, 1.0, 0.0).astype(F32)
    upper = jnp.where(row_at <= column_at, 1.0, 0.0).astype(F32)
    first_head = lax.broadcasted_iota(jnp.int32, (1, GROUP), 1) < head_width
    same_head = jnp.where(row_at // head_width == column_at // head_width, 1.0, 0.0).astype(BF16)
    same_head_twice = jnp.concatenate([same_head, same_head], axis=0)

    def project(slab, first_column):
        columns = pl.ds(first_column, CHUNK)
        matrix = slabs[slab].reshape(width, CHUNK)
        projected[...] = (
            jnp.dot(normed[...], matrix, preferred_element_type=F32).astype(BF16).astype(F32)
        )
        taps = conv_weight_ref.shape[0]
        for block in range(block_count):
            total = bias_held[slab]
            for tap in range(taps):
                first = HALO + block * GROUP + tap - (taps - 1)
                total = total + conv_weight_ref[tap : tap + 1, columns] * projected[
                    first : first + GROUP, :
                ]
            mixed[block * GROUP : (block + 1) * GROUP, :] = (
                0.5 * total * (1.0 + jnp.tanh(0.5 * total))
            ).astype(BF16)

    def both(columns, pair):
        return jnp.where(
            first_head, columns[:, 2 * pair : 2 * pair + 1], columns[:, 2 * pair + 1 : 2 * pair + 2]
        )

    pass_x(0)
    for slab in range(slab_count):
        first = chunk_count * CHUNK if slab == 0 else (slab - 1) * CHUNK
        bias_held[slab] = conv_bias_ref[first : first + CHUNK].reshape(1, CHUNK)
    for chunk in range(chunk_count):
        for pair in range(head_count // 2):
            head = chunk * head_count + 2 * pair
            skip_held[chunk, :, pair * GROUP : (pair + 1) * GROUP] = jnp.where(
                first_head, skip_ref[:, head : head + 1], skip_ref[:, head + 1 : head + 2]
            )
    for block in range(block_count):
        rows = slice(block * GROUP, (block + 1) * GROUP)
        decay = decay_ref[:, rows]
        across = jnp.dot(decay, upper, precision=lax.Precision.HIGHEST, preferred_element_type=F32)
        turned = (((1,), (1,)), ((), ()))
        down = lax.dot_general(
            lower, decay, turned, precision=lax.Precision.HIGHEST, preferred_element_type=F32
        )
        down_decay = lax.dot_general(
            unit, decay, turned, precision=lax.Precision.HIGHEST, preferred_element_type=F32
        )
        for chunk in range(chunk_count):
            heads = slice(chunk * head_count, (chunk + 1) * head_count)
            down_held[chunk, rows, :head_count] = down[:, heads]
            down_decay_held[chunk, rows, :head_count] = down_decay[:, heads]
            across_held[chunk, :head_count, rows] = across[heads, :]
            decay_held[chunk, :head_count, rows] = decay[heads, :]
    pass_core(0)
    pass_x(1)
    choice[...] = jnp.transpose(
        jnp.where(
            lax.broadcasted_iota(jnp.int32, (positions, positions), 0) == order_ref[...], 1.0, 0.0
        ).astype(F32)
    ).astype(BF16)

    @pl.when(seq > 0)
    def _():
        halo_copy.wait_recv()

    whole_slab(0)
    project(0, chunk_count * CHUNK)
    pass_x(2)
    pass_core(1)
    for block in range(block_count):
        rows = slice(block * GROUP, (block + 1) * GROUP)
        b_block = mixed[rows, :GROUP]
        c_block = mixed[rows, GROUP:]
        c_held[block] = c_block
        b_turned[block] = jnp.transpose(b_block.astype(F32)).astype(BF16)
        scores[block] = jnp.where(
            causal, jnp.dot(c_block, b_turned[block], preferred_element_type=F32), 0.0
        )
    def state_copy(chunk):
        return pltpu.make_async_remote_copy(
            src_ref=leaving_state.at[chunk],
            dst_ref=arriving_state.at[chunk],
            send_sem=state_send.at[chunk],
            recv_sem=state_recv.at[chunk],
            device_id=(dp, (seq + 1) % seq_count),
            device_id_type=MESH,
        )

    def out_columns(chunk):
        return pl.ds(pl.multiple_of(chunk * CHUNK, CHUNK), CHUNK)

    def out_copy(chunk, k, source):
        target = (seq + k) % seq_count
        return pltpu.make_async_remote_copy(
            src_ref=picked.at[chunk, pl.ds(pl.multiple_of(target * share, share), share)],
            dst_ref=arrived.at[chunk, source],
            send_sem=out_send.at[chunk, k - 1],
            recv_sem=out_recv.at[chunk, k - 1],
            device_id=(dp, target),
            device_id_type=MESH,
        )

    step = min(share, max(GROUP // seq_count, 16))
    mixed_rows = step * seq_count
    row = lax.broadcasted_iota(jnp.int32, (mixed_rows, mixed_rows), 0)
    column = lax.broadcasted_iota(jnp.int32, (mixed_rows, mixed_rows), 1)
    frame = column // step
    frames_within = jnp.where(
        row == (column - frame * step) * seq_count + frame, 1.0, 0.0
    ).astype(BF16)

    def finish(chunk):
        for k in range(1, seq_count):
            out_copy(chunk, k, (seq + seq_count - k) % seq_count).wait_recv()
        for first in range(0, share, step):
            block = jnp.concatenate(
                [arrived[chunk, f, first : first + step, :] for f in range(seq_count)], axis=0
            )
            together[chunk, first * seq_count : first * seq_count + mixed_rows, :] = jnp.dot(
                frames_within, block, preferred_element_type=F32
            ).astype(BF16)
        pltpu.make_async_copy(
            together.at[chunk], result_ref.at[:, out_columns(chunk)], own_sem.at[chunk]
        ).start()

    def work(chunk, carry):
        slab = chunk + 1

        whole_slab(slab)
        project(slab, pl.multiple_of(chunk * CHUNK, CHUNK))

        @pl.when(slab + 2 < slab_count)
        def _():
            pass_x(slab + 2)

        fadings = []
        for block in range(block_count):
            rows = slice(block * GROUP, (block + 1) * GROUP)
            decay = decay_held[chunk, :head_count, rows]
            across = across_held[chunk, :head_count, rows]
            down = down_held[chunk, rows, :head_count]
            closing = down[GROUP - 1 : GROUP, :]
            scale = jnp.exp(closing - down) * (-down_decay_held[chunk, rows, :head_count])
            fading = jnp.exp(closing)
            grown = jnp.exp(down)
            fades = []
            for pair in range(head_count // 2):
                lanes = slice(pair * GROUP, (pair + 1) * GROUP)
                x_pair = mixed[rows, lanes]
                x_wide = x_pair.astype(F32)
                weights = []
                for head in (2 * pair, 2 * pair + 1):
                    gap = down[:, head : head + 1] - across[head : head + 1, :]
                    weights.append(
                        (
                            scores[block]
                            * jnp.exp(jnp.minimum(gap, 0.0))
                            * (-decay[head : head + 1, :])
                        ).astype(BF16)
                    )
                x_apart = jnp.concatenate(
                    [jnp.where(first_head, x_wide, 0.0), jnp.where(first_head, 0.0, x_wide)], axis=0
                ).astype(BF16)
                intra[rows, lanes] = (
                    jnp.dot(
                        jnp.concatenate(weights, axis=1), x_apart, preferred_element_type=F32
                    )
                    + skip_held[chunk, :, lanes] * x_wide
                )
                scaled = (both(scale, pair) * x_wide).astype(BF16)
                block_states[block, :, lanes] = jnp.dot(
                    b_turned[block], scaled, preferred_element_type=F32
                )
                expanded[rows, lanes] = both(grown, pair)
                fades.append(both(fading, pair))
            fadings.append(jnp.concatenate(fades, axis=1))

        @pl.when(slab + 1 < slab_count)
        def _():
            pass_core(slab + 1)

        @pl.when(slab + 2 < slab_count)
        def _():
            pass_y(slab + 2)

        @pl.when(seq > 0)
        def _():
            state_copy(chunk).wait_recv()

        @pl.when(seq == 0)
        def _():
            arriving_state[chunk] = jnp.zeros(arriving_state.shape[1:], F32)

        state = arriving_state[chunk]
        for block in range(block_count):
            entering_half[block] = state.astype(BF16)
            state = fadings[block] * state + block_states[block]
        leaving_state[chunk] = state

        @pl.when(seq < seq_count - 1)
        def _():
            state_copy(chunk).start()

        gains = out_gain_ref[:, out_columns(chunk)]
        for block in range(block_count):
            rows = slice(block * GROUP, (block + 1) * GROUP)
            inter = jnp.dot(c_held[block], entering_half[block], preferred_element_type=F32)
            ssm = intra[rows, :] + inter * expanded[rows, :]
            square = ssm * ssm
            high = square.astype(BF16)
            low = (square - high.astype(F32)).astype(BF16)
            for pair in range(head_count // 2):
                lanes = slice(pair * GROUP, (pair + 1) * GROUP)
                total = jnp.dot(
                    jnp.concatenate([high[:, lanes], low[:, lanes]], axis=1),
                    same_head_twice,
                    preferred_element_type=F32,
                )
                head_scale = lax.rsqrt(total * (1.0 / head_width) + 1e-05)
                normalized[rows, lanes] = (
                    ssm[:, lanes] * head_scale * gains[:, lanes]
                ).astype(BF16)
        picked[chunk] = jnp.dot(choice[...], normalized[...], preferred_element_type=F32).astype(BF16)
        for k in range(1, seq_count):
            out_copy(chunk, k, seq).start()
        arrived[chunk, seq] = picked[chunk, pl.ds(pl.multiple_of(seq * share, share), share)]

        @pl.when(chunk >= LAG)
        def _():
            finish(chunk - LAG)

        return carry

    lax.fori_loop(0, chunk_count, work, 0)

    for chunk in range(max(chunk_count - LAG, 0), chunk_count):
        finish(chunk)

    def out_settle(chunk, carry):
        for k in range(1, seq_count):
            out_copy(chunk, k, seq).wait_send()
        pltpu.make_async_copy(
            together.at[chunk], result_ref.at[:, out_columns(chunk)], own_sem.at[chunk]
        ).wait()
        return carry

    lax.fori_loop(0, chunk_count, out_settle, 0)

    def settle(slab, carry):
        for k in range(1, z_count):
            where_carried(slab, z, z_copy(slab, k, z).wait_send)
        for k in range(1, x_count):
            where_split(
                slab, x_copy(slab, k, x, "plane").wait_send, x_copy(slab, k, x, None).wait_send
            )

        def y_settle():
            for k in range(1, planes):
                y_copy(slab, k, plane).wait_send()

        where_true(is_split(slab), y_settle)
        if core_count > 1:
            core_copy(slab, core).wait_send()
        return carry

    lax.fori_loop(0, slab_count, settle, 0)

    @pl.when(seq < seq_count - 1)
    def _():
        halo_copy.wait_send()

        def state_settle(chunk, carry):
            state_copy(chunk).wait_send()
            return carry

        lax.fori_loop(0, chunk_count, state_settle, 0)


def on_device(
    sizes, tokens, in_gain, in_weight, conv_weight, conv_bias, log_decay, skip, out_gain, scan_order
):
    z_count, x_count, core_count, seq_count = sizes
    token_count, width = tokens.shape[1:]
    own_rows, channels = in_weight.shape
    heads = log_decay.shape[1]
    inner = out_gain.shape[0]
    head_width = inner // heads
    chunk_count = inner // CHUNK
    slab_count = chunk_count + 1
    per_chunk = heads // chunk_count
    taps = conv_weight.shape[0]
    positions = scan_order.shape[0]
    share = positions // seq_count
    assert token_count == positions and channels == inner + 2 * GROUP and per_chunk == 4

    block_count = token_count // GROUP
    planes = seq_count // core_count
    if z_count % planes:
        planes = 1
    hops = max(z_count - 1, 1), max(x_count - 1, 1), max(seq_count - 1, 1)
    regrouped = pl.pallas_call(
        functools.partial(fused_kernel, sizes + (head_width,)),
        out_shape=jax.ShapeDtypeStruct((token_count, inner), BF16),
        in_specs=[pl.BlockSpec(memory_space=pl.ANY)] * 9,
        out_specs=pl.BlockSpec(memory_space=pl.ANY),
        scratch_shapes=[
            pltpu.VMEM((token_count, width), BF16),
            pltpu.VMEM((1, width), F32),
            pltpu.VMEM((taps, channels), F32),
            pltpu.VMEM((channels,), F32),
            pltpu.VMEM((heads, token_count), F32),
            pltpu.VMEM((1, heads), F32),
            pltpu.VMEM((1, inner), F32),
            pltpu.VMEM((1, positions), jnp.int32),
            pltpu.VMEM((chunk_count, 1, CHUNK), F32),
            pltpu.VMEM((slab_count, 1, CHUNK), F32),
            pltpu.VMEM((chunk_count, seq_count, share, CHUNK), BF16),
            pltpu.VMEM((chunk_count, positions, CHUNK), BF16),
            pltpu.VMEM(
                (
                    slab_count,
                    z_count // planes,
                    planes,
                    x_count,
                    core_count,
                    own_rows // core_count,
                    CHUNK,
                ),
                BF16,
            ),
            pltpu.VMEM((HALO + token_count, width), BF16),
            pltpu.VMEM((positions, positions), BF16),
            pltpu.VMEM((chunk_count, token_count, GROUP), F32),
            pltpu.VMEM((chunk_count, token_count, GROUP), F32),
            pltpu.VMEM((chunk_count, 8, token_count), F32),
            pltpu.VMEM((chunk_count, 8, token_count), F32),
            pltpu.VMEM((HALO + token_count, CHUNK), F32),
            pltpu.VMEM((token_count, CHUNK), BF16),
            pltpu.VMEM((token_count // GROUP, GROUP, GROUP), BF16),
            pltpu.VMEM((token_count // GROUP, GROUP, GROUP), BF16),
            pltpu.VMEM((token_count // GROUP, GROUP, GROUP), F32),
            pltpu.VMEM((token_count // GROUP, GROUP, CHUNK), F32),
            pltpu.VMEM((token_count // GROUP, GROUP, CHUNK), BF16),
            pltpu.VMEM((token_count, CHUNK), F32),
            pltpu.VMEM((token_count, CHUNK), F32),
            pltpu.VMEM((chunk_count, GROUP, CHUNK), F32),
            pltpu.VMEM((chunk_count, GROUP, CHUNK), F32),
            pltpu.VMEM((token_count, CHUNK), BF16),
            pltpu.VMEM((chunk_count, positions, CHUNK), BF16),
            pltpu.SemaphoreType.DMA((slab_count, hops[0])),
            pltpu.SemaphoreType.DMA((slab_count, hops[0])),
            pltpu.SemaphoreType.DMA((slab_count, hops[1])),
            pltpu.SemaphoreType.DMA((slab_count, hops[1])),
            pltpu.SemaphoreType.DMA((slab_count // SPLIT, max(planes - 1, 1))),
            pltpu.SemaphoreType.DMA((slab_count // SPLIT, max(planes - 1, 1))),
            pltpu.SemaphoreType.DMA((slab_count,)),
            pltpu.SemaphoreType.DMA((slab_count,)),
            pltpu.SemaphoreType.DMA,
            pltpu.SemaphoreType.DMA,
            pltpu.SemaphoreType.DMA((chunk_count,)),
            pltpu.SemaphoreType.DMA((chunk_count,)),
            pltpu.SemaphoreType.DMA((chunk_count, hops[2])),
            pltpu.SemaphoreType.DMA((chunk_count, hops[2])),
            pltpu.SemaphoreType.DMA((chunk_count,)),
            pltpu.SemaphoreType.DMA((block_count,)),
            pltpu.SemaphoreType.DMA((slab_count,)),
            pltpu.SemaphoreType.DMA((7,)),
        ],
        compiler_params=pltpu.CompilerParams(
            collective_id=0, has_side_effects=True, vmem_limit_bytes=58 * 1024 * 1024
        ),
        name="projected_scan",
    )(
        tokens[0],
        in_gain.reshape(1, width),
        in_weight,
        conv_weight,
        conv_bias,
        log_decay[0],
        skip.reshape(1, heads),
        out_gain.reshape(1, inner),
        scan_order.reshape(1, positions),
    )
    return regrouped[None]


def solution(mesh):
    dp_count, seq_count = mesh.shape["dp"], mesh.shape["seq"]
    x_count = 2 ** (int(math.log2(dp_count)) // 2)
    while dp_count % x_count:
        x_count //= 2
    sizes = (dp_count // x_count, x_count, 2 if seq_count % 2 == 0 else 1, seq_count)
    in_specs = (
        P("dp", "seq", None),
        P(),
        P("dp", None),
        P(),
        P(),
        P("dp", None, "seq"),
        P(),
        P(),
        P(),
    )
    return jax.shard_map(
        functools.partial(on_device, sizes),
        mesh=mesh,
        in_specs=in_specs,
        out_specs=P("dp", "seq", None),
        check_vma=False,
    )
```

```python
import functools
import math

import jax
import jax.numpy as jnp
from jax import lax
from jax.experimental import pallas as pl
from jax.experimental.pallas import tpu as pltpu
from jax.sharding import PartitionSpec as P

GROUP = 128
CHUNK = 256
HALO = 16
WINDOW = 3
SPLIT = 2
LAG = 2
BF16 = jnp.bfloat16
F32 = jnp.float32
MESH = pl.DeviceIdType.MESH


def fused_kernel(
    sizes,
    tokens_hbm,
    gain_hbm,
    weight_hbm,
    conv_weight_hbm,
    conv_bias_hbm,
    decay_hbm,
    skip_hbm,
    out_gain_hbm,
    order_hbm,
    result_ref,
    tokens_ref,
    gain_ref,
    conv_weight_ref,
    conv_bias_ref,
    decay_ref,
    skip_ref,
    out_gain_ref,
    order_ref,
    skip_held,
    bias_held,
    arrived,
    together,
    slabs,
    normed,
    choice,
    down_held,
    down_decay_held,
    across_held,
    decay_held,
    projected,
    mixed,
    b_turned,
    c_held,
    scores,
    block_states,
    entering_half,
    intra,
    expanded,
    arriving_state,
    leaving_state,
    normalized,
    picked,
    z_send,
    z_recv,
    x_send,
    x_recv,
    y_send,
    y_recv,
    core_send,
    core_recv,
    halo_send,
    halo_recv,
    state_send,
    state_recv,
    out_send,
    out_recv,
    own_sem,
    token_sem,
    weight_sem,
    small_sem,
):
    z_count, x_count, core_count, seq_count, head_width = sizes
    head_count = CHUNK // head_width
    dp = lax.axis_index("dp")
    seq = lax.axis_index("seq")
    z = dp // x_count
    x = dp % x_count
    core = seq % core_count
    planes = slabs.shape[2]
    plane = seq // core_count % planes
    sibling = seq - core + (core + 1) % core_count
    half = slabs.shape[5]
    slab_count = slabs.shape[0]
    chunk_count = slab_count - 1
    token_count, width = tokens_ref.shape
    block_count = token_count // GROUP
    positions = order_ref.shape[1]
    share = positions // seq_count

    partners = [(((z + k) % z_count) * x_count + x, seq) for k in range(1, z_count)]
    partners += [(z * x_count + (x + k) % x_count, seq) for k in range(1, x_count)]
    partners += [(dp, (seq + k) % seq_count) for k in range(1, seq_count)]
    barrier = pltpu.get_barrier_semaphore()
    for partner in partners:
        pl.semaphore_signal(barrier, inc=1, device_id=partner, device_id_type=MESH)

    def is_split(slab):
        if planes == 1:
            return False
        if isinstance(slab, int):
            return 0 < slab <= SPLIT
        return jnp.logical_and(slab > 0, slab <= SPLIT)

    def where_true(condition, act):
        if isinstance(condition, bool):
            if condition:
                act()
        else:
            pl.when(condition)(act)

    def where_carried(slab, row, act):
        split = is_split(slab)
        if split is False:
            act()
        else:
            pl.when(jnp.logical_or(jnp.logical_not(split), row % planes == plane))(act)

    own_rows = pl.ds(pl.multiple_of(core * half, half), half)

    def load_weight(slab):
        first = chunk_count * CHUNK if slab == 0 else (slab - 1) * CHUNK
        return pltpu.make_async_copy(
            weight_hbm.at[own_rows, first : first + CHUNK],
            slabs.at[slab, z // planes, z % planes, x, core],
            weight_sem.at[slab],
        )

    def load_tokens(block):
        rows = slice(block * GROUP, (block + 1) * GROUP)
        return pltpu.make_async_copy(tokens_hbm.at[rows], tokens_ref.at[rows], token_sem.at[block])

    small = [
        pltpu.make_async_copy(source, target, small_sem.at[i])
        for i, (source, target) in enumerate(
            [
                (gain_hbm, gain_ref),
                (conv_weight_hbm, conv_weight_ref),
                (conv_bias_hbm, conv_bias_ref),
                (decay_hbm, decay_ref),
                (skip_hbm, skip_ref),
                (out_gain_hbm, out_gain_ref),
                (order_hbm, order_ref),
            ]
        )
    ]
    for slab in range(slab_count):
        where_carried(slab, z, load_weight(slab).start)
    for block in range(block_count):
        load_tokens(block).start()
    for copy in small:
        copy.start()
    for slab in range(slab_count):
        where_carried(slab, z, load_weight(slab).wait)
    pl.semaphore_wait(barrier, len(partners))

    def z_copy(slab, k, source):
        return pltpu.make_async_remote_copy(
            src_ref=slabs.at[slab, source // planes, source % planes, x, core],
            dst_ref=slabs.at[slab, source // planes, source % planes, x, core],
            send_sem=z_send.at[slab, k - 1],
            recv_sem=z_recv.at[slab, k - 1],
            device_id=(((z + k) % z_count) * x_count + x, seq),
            device_id_type=MESH,
        )

    def x_copy(slab, k, source, row):
        if row is None:
            piece = slabs.at[slab, :, :, source, core]
        elif isinstance(row, str):
            piece = slabs.at[slab, :, plane, source, core]
        else:
            piece = slabs.at[slab, row // planes, row % planes, source, core]
        return pltpu.make_async_remote_copy(
            src_ref=piece,
            dst_ref=piece,
            send_sem=x_send.at[slab, k - 1],
            recv_sem=x_recv.at[slab, k - 1],
            device_id=(z * x_count + (x + k) % x_count, seq),
            device_id_type=MESH,
        )

    def core_copy(slab, source):
        return pltpu.make_async_remote_copy(
            src_ref=slabs.at[slab, :, :, :, source],
            dst_ref=slabs.at[slab, :, :, :, source],
            send_sem=core_send.at[slab],
            recv_sem=core_recv.at[slab],
            device_id=(dp, sibling),
            device_id_type=MESH,
        )

    def y_copy(slab, k, source):
        piece = slabs.at[slab, :, source, :, core]
        return pltpu.make_async_remote_copy(
            src_ref=piece,
            dst_ref=piece,
            send_sem=y_send.at[slab - 1, k - 1],
            recv_sem=y_recv.at[slab - 1, k - 1],
            device_id=(dp, (plane + k) % planes * core_count + core),
            device_id_type=MESH,
        )

    def where_split(slab, act, otherwise):
        split = is_split(slab)
        where_true(split, act)
        where_true(not split if isinstance(split, bool) else jnp.logical_not(split), otherwise)

    def send_own(slab):
        def act():
            for k in range(1, z_count):
                z_copy(slab, k, z).start()
            for k in range(1, x_count):
                x_copy(slab, k, x, z).start()

        where_carried(slab, z, act)

    def pass_x(slab):
        for k in range(1, z_count):
            row = (z + z_count - k) % z_count

            def act(k=k, row=row):
                z_copy(slab, k, row).wait_recv()
                for kx in range(1, x_count):
                    x_copy(slab, kx, x, row).start()

            where_carried(slab, row, act)

        if isinstance(slab, int):
            if slab + WINDOW < slab_count:
                send_own(slab + WINDOW)
        else:

            @pl.when(slab + WINDOW < slab_count)
            def _():
                send_own(slab + WINDOW)

    def x_arrived(slab, rows):
        for k in range(1, x_count):
            x_copy(slab, k, (x + x_count - k) % x_count, rows).wait_recv()

    def pass_y(slab):
        def act():
            x_arrived(slab, "plane")
            for k in range(1, planes):
                y_copy(slab, k, plane).start()

        where_true(is_split(slab), act)

    def pass_core(slab):
        def y_arrived():
            for k in range(1, planes):
                y_copy(slab, k, (plane + planes - k) % planes).wait_recv()

        where_split(slab, y_arrived, lambda: x_arrived(slab, None))
        if core_count > 1:
            core_copy(slab, core).start()

    def whole_slab(slab):
        if core_count > 1:
            core_copy(slab, (core + 1) % core_count).wait_recv()

    for slab in range(min(WINDOW, slab_count)):
        send_own(slab)

    for copy in small:
        copy.wait()
    for block in range(block_count):
        load_tokens(block).wait()
        rows = tokens_ref[block * GROUP : (block + 1) * GROUP, :].astype(F32)
        inverse = lax.rsqrt(jnp.mean(rows * rows, axis=1, keepdims=True) + 1e-05)
        normed[HALO + block * GROUP : HALO + (block + 1) * GROUP, :] = (
            rows * inverse * gain_ref[...]
        ).astype(BF16)

    halo_copy = pltpu.make_async_remote_copy(
        src_ref=normed.at[token_count : token_count + HALO],
        dst_ref=normed.at[0:HALO],
        send_sem=halo_send,
        recv_sem=halo_recv,
        device_id=(dp, (seq + 1) % seq_count),
        device_id_type=MESH,
    )

    @pl.when(seq < seq_count - 1)
    def _():
        halo_copy.start()

    @pl.when(seq == 0)
    def _():
        normed[0:HALO, :] = jnp.zeros((HALO, width), BF16)

    row_at = lax.broadcasted_iota(jnp.int32, (GROUP, GROUP), 0)
    column_at = lax.broadcasted_iota(jnp.int32, (GROUP, GROUP), 1)
    causal = column_at <= row_at
    lower = jnp.where(causal, 1.0, 0.0).astype(F32)
    unit = jnp.where(row_at == column_at, 1.0, 0.0).astype(F32)
    upper = jnp.where(row_at <= column_at, 1.0, 0.0).astype(F32)
    first_head = lax.broadcasted_iota(jnp.int32, (1, GROUP), 1) < head_width
    same_head = jnp.where(row_at // head_width == column_at // head_width, 1.0, 0.0).astype(BF16)
    same_head_twice = jnp.concatenate([same_head, same_head], axis=0)

    def project(slab, first_column):
        columns = pl.ds(first_column, CHUNK)
        matrix = slabs[slab].reshape(width, CHUNK)
        projected[...] = (
            jnp.dot(normed[...], matrix, preferred_element_type=F32).astype(BF16).astype(F32)
        )
        taps = conv_weight_ref.shape[0]
        for block in range(block_count):
            total = bias_held[slab]
            for tap in range(taps):
                first = HALO + block * GROUP + tap - (taps - 1)
                total = total + conv_weight_ref[tap : tap + 1, columns] * projected[
                    first : first + GROUP, :
                ]
            mixed[block * GROUP : (block + 1) * GROUP, :] = (
                0.5 * total * (1.0 + jnp.tanh(0.5 * total))
            ).astype(BF16)

    def both(columns, pair):
        return jnp.where(
            first_head, columns[:, 2 * pair : 2 * pair + 1], columns[:, 2 * pair + 1 : 2 * pair + 2]
        )

    pass_x(0)
    for slab in range(slab_count):
        first = chunk_count * CHUNK if slab == 0 else (slab - 1) * CHUNK
        bias_held[slab] = conv_bias_ref[first : first + CHUNK].reshape(1, CHUNK)
    for chunk in range(chunk_count):
        for pair in range(head_count // 2):
            head = chunk * head_count + 2 * pair
            skip_held[chunk, :, pair * GROUP : (pair + 1) * GROUP] = jnp.where(
                first_head, skip_ref[:, head : head + 1], skip_ref[:, head + 1 : head + 2]
            )
    for block in range(block_count):
        rows = slice(block * GROUP, (block + 1) * GROUP)
        decay = decay_ref[:, rows]
        across = jnp.dot(decay, upper, precision=lax.Precision.HIGHEST, preferred_element_type=F32)
        turned = (((1,), (1,)), ((), ()))
        down = lax.dot_general(
            lower, decay, turned, precision=lax.Precision.HIGHEST, preferred_element_type=F32
        )
        down_decay = lax.dot_general(
            unit, decay, turned, precision=lax.Precision.HIGHEST, preferred_element_type=F32
        )
        for chunk in range(chunk_count):
            heads = slice(chunk * head_count, (chunk + 1) * head_count)
            down_held[chunk, rows, :head_count] = down[:, heads]
            down_decay_held[chunk, rows, :head_count] = down_decay[:, heads]
            across_held[chunk, :head_count, rows] = across[heads, :]
            decay_held[chunk, :head_count, rows] = decay[heads, :]
    pass_core(0)
    pass_x(1)
    pass_y(1)
    choice[...] = jnp.transpose(
        jnp.where(
            lax.broadcasted_iota(jnp.int32, (positions, positions), 0) == order_ref[...], 1.0, 0.0
        ).astype(F32)
    ).astype(BF16)

    @pl.when(seq > 0)
    def _():
        halo_copy.wait_recv()

    whole_slab(0)
    project(0, chunk_count * CHUNK)
    pass_x(2)
    pass_y(2)
    for block in range(block_count):
        rows = slice(block * GROUP, (block + 1) * GROUP)
        b_block = mixed[rows, :GROUP]
        c_block = mixed[rows, GROUP:]
        c_held[block] = c_block
        b_turned[block] = jnp.transpose(b_block.astype(F32)).astype(BF16)
        scores[block] = jnp.where(
            causal, jnp.dot(c_block, b_turned[block], preferred_element_type=F32), 0.0
        )
    pass_core(1)

    def state_copy(chunk):
        return pltpu.make_async_remote_copy(
            src_ref=leaving_state.at[chunk],
            dst_ref=arriving_state.at[chunk],
            send_sem=state_send.at[chunk],
            recv_sem=state_recv.at[chunk],
            device_id=(dp, (seq + 1) % seq_count),
            device_id_type=MESH,
        )

    def out_columns(chunk):
        return pl.ds(pl.multiple_of(chunk * CHUNK, CHUNK), CHUNK)

    def out_copy(chunk, k, source):
        target = (seq + k) % seq_count
        return pltpu.make_async_remote_copy(
            src_ref=picked.at[chunk, pl.ds(pl.multiple_of(target * share, share), share)],
            dst_ref=arrived.at[chunk, source],
            send_sem=out_send.at[chunk, k - 1],
            recv_sem=out_recv.at[chunk, k - 1],
            device_id=(dp, target),
            device_id_type=MESH,
        )

    step = min(share, max(GROUP // seq_count, 16))
    mixed_rows = step * seq_count
    row = lax.broadcasted_iota(jnp.int32, (mixed_rows, mixed_rows), 0)
    column = lax.broadcasted_iota(jnp.int32, (mixed_rows, mixed_rows), 1)
    frame = column // step
    frames_within = jnp.where(
        row == (column - frame * step) * seq_count + frame, 1.0, 0.0
    ).astype(BF16)

    def finish(chunk):
        for k in range(1, seq_count):
            out_copy(chunk, k, (seq + seq_count - k) % seq_count).wait_recv()
        for first in range(0, share, step):
            block = jnp.concatenate(
                [arrived[chunk, f, first : first + step, :] for f in range(seq_count)], axis=0
            )
            together[chunk, first * seq_count : first * seq_count + mixed_rows, :] = jnp.dot(
                frames_within, block, preferred_element_type=F32
            ).astype(BF16)
        pltpu.make_async_copy(
            together.at[chunk], result_ref.at[:, out_columns(chunk)], own_sem.at[chunk]
        ).start()

    def work(chunk, carry):
        slab = chunk + 1

        whole_slab(slab)
        project(slab, pl.multiple_of(chunk * CHUNK, CHUNK))

        @pl.when(slab + 2 < slab_count)
        def _():
            pass_x(slab + 2)

        fadings = []
        for block in range(block_count):
            rows = slice(block * GROUP, (block + 1) * GROUP)
            decay = decay_held[chunk, :head_count, rows]
            across = across_held[chunk, :head_count, rows]
            down = down_held[chunk, rows, :head_count]
            closing = down[GROUP - 1 : GROUP, :]
            scale = jnp.exp(closing - down) * (-down_decay_held[chunk, rows, :head_count])
            fading = jnp.exp(closing)
            grown = jnp.exp(down)
            fades = []
            for pair in range(head_count // 2):
                lanes = slice(pair * GROUP, (pair + 1) * GROUP)
                x_pair = mixed[rows, lanes]
                x_wide = x_pair.astype(F32)
                weights = []
                for head in (2 * pair, 2 * pair + 1):
                    gap = down[:, head : head + 1] - across[head : head + 1, :]
                    weights.append(
                        (
                            scores[block]
                            * jnp.exp(jnp.minimum(gap, 0.0))
                            * (-decay[head : head + 1, :])
                        ).astype(BF16)
                    )
                x_apart = jnp.concatenate(
                    [jnp.where(first_head, x_wide, 0.0), jnp.where(first_head, 0.0, x_wide)], axis=0
                ).astype(BF16)
                intra[rows, lanes] = (
                    jnp.dot(
                        jnp.concatenate(weights, axis=1), x_apart, preferred_element_type=F32
                    )
                    + skip_held[chunk, :, lanes] * x_wide
                )
                scaled = (both(scale, pair) * x_wide).astype(BF16)
                block_states[block, :, lanes] = jnp.dot(
                    b_turned[block], scaled, preferred_element_type=F32
                )
                expanded[rows, lanes] = both(grown, pair)
                fades.append(both(fading, pair))
            fadings.append(jnp.concatenate(fades, axis=1))

        @pl.when(slab + 1 < slab_count)
        def _():
            pass_core(slab + 1)

        @pl.when(seq > 0)
        def _():
            state_copy(chunk).wait_recv()

        @pl.when(seq == 0)
        def _():
            arriving_state[chunk] = jnp.zeros(arriving_state.shape[1:], BF16)

        state = arriving_state[chunk].astype(F32)
        for block in range(block_count):
            entering_half[block] = state.astype(BF16)
            state = fadings[block] * state + block_states[block]
        leaving_state[chunk] = state.astype(BF16)

        @pl.when(seq < seq_count - 1)
        def _():
            state_copy(chunk).start()

        gains = out_gain_ref[:, out_columns(chunk)]
        for block in range(block_count):
            rows = slice(block * GROUP, (block + 1) * GROUP)
            inter = jnp.dot(c_held[block], entering_half[block], preferred_element_type=F32)
            ssm = intra[rows, :] + inter * expanded[rows, :]
            square = ssm * ssm
            high = square.astype(BF16)
            low = (square - high.astype(F32)).astype(BF16)
            for pair in range(head_count // 2):
                lanes = slice(pair * GROUP, (pair + 1) * GROUP)
                total = jnp.dot(
                    jnp.concatenate([high[:, lanes], low[:, lanes]], axis=1),
                    same_head_twice,
                    preferred_element_type=F32,
                )
                head_scale = lax.rsqrt(total * (1.0 / head_width) + 1e-05)
                normalized[rows, lanes] = (
                    ssm[:, lanes] * head_scale * gains[:, lanes]
                ).astype(BF16)
        picked[chunk] = jnp.dot(choice[...], normalized[...], preferred_element_type=F32).astype(BF16)
        for k in range(1, seq_count):
            out_copy(chunk, k, seq).start()
        arrived[chunk, seq] = picked[chunk, pl.ds(pl.multiple_of(seq * share, share), share)]

        @pl.when(chunk >= LAG)
        def _():
            finish(chunk - LAG)

        return carry

    lax.fori_loop(0, chunk_count, work, 0)

    for chunk in range(max(chunk_count - LAG, 0), chunk_count):
        finish(chunk)

    def out_settle(chunk, carry):
        for k in range(1, seq_count):
            out_copy(chunk, k, seq).wait_send()
        pltpu.make_async_copy(
            together.at[chunk], result_ref.at[:, out_columns(chunk)], own_sem.at[chunk]
        ).wait()
        return carry

    lax.fori_loop(0, chunk_count, out_settle, 0)

    def settle(slab, carry):
        for k in range(1, z_count):
            where_carried(slab, z, z_copy(slab, k, z).wait_send)
        for k in range(1, x_count):
            where_split(
                slab, x_copy(slab, k, x, "plane").wait_send, x_copy(slab, k, x, None).wait_send
            )

        def y_settle():
            for k in range(1, planes):
                y_copy(slab, k, plane).wait_send()

        where_true(is_split(slab), y_settle)
        if core_count > 1:
            core_copy(slab, core).wait_send()
        return carry

    lax.fori_loop(0, slab_count, settle, 0)

    @pl.when(seq < seq_count - 1)
    def _():
        halo_copy.wait_send()

        def state_settle(chunk, carry):
            state_copy(chunk).wait_send()
            return carry

        lax.fori_loop(0, chunk_count, state_settle, 0)


def on_device(
    sizes, tokens, in_gain, in_weight, conv_weight, conv_bias, log_decay, skip, out_gain, scan_order
):
    z_count, x_count, core_count, seq_count = sizes
    token_count, width = tokens.shape[1:]
    own_rows, channels = in_weight.shape
    heads = log_decay.shape[1]
    inner = out_gain.shape[0]
    head_width = inner // heads
    chunk_count = inner // CHUNK
    slab_count = chunk_count + 1
    per_chunk = heads // chunk_count
    taps = conv_weight.shape[0]
    positions = scan_order.shape[0]
    share = positions // seq_count
    assert token_count == positions and channels == inner + 2 * GROUP and per_chunk == 4

    block_count = token_count // GROUP
    planes = seq_count // core_count
    if z_count % planes:
        planes = 1
    hops = max(z_count - 1, 1), max(x_count - 1, 1), max(seq_count - 1, 1)
    regrouped = pl.pallas_call(
        functools.partial(fused_kernel, sizes + (head_width,)),
        out_shape=jax.ShapeDtypeStruct((token_count, inner), BF16),
        in_specs=[pl.BlockSpec(memory_space=pl.ANY)] * 9,
        out_specs=pl.BlockSpec(memory_space=pl.ANY),
        scratch_shapes=[
            pltpu.VMEM((token_count, width), BF16),
            pltpu.VMEM((1, width), F32),
            pltpu.VMEM((taps, channels), F32),
            pltpu.VMEM((channels,), F32),
            pltpu.VMEM((heads, token_count), F32),
            pltpu.VMEM((1, heads), F32),
            pltpu.VMEM((1, inner), F32),
            pltpu.VMEM((1, positions), jnp.int32),
            pltpu.VMEM((chunk_count, 1, CHUNK), F32),
            pltpu.VMEM((slab_count, 1, CHUNK), F32),
            pltpu.VMEM((chunk_count, seq_count, share, CHUNK), BF16),
            pltpu.VMEM((chunk_count, positions, CHUNK), BF16),
            pltpu.VMEM(
                (
                    slab_count,
                    z_count // planes,
                    planes,
                    x_count,
                    core_count,
                    own_rows // core_count,
                    CHUNK,
                ),
                BF16,
            ),
            pltpu.VMEM((HALO + token_count, width), BF16),
            pltpu.VMEM((positions, positions), BF16),
            pltpu.VMEM((chunk_count, token_count, GROUP), F32),
            pltpu.VMEM((chunk_count, token_count, GROUP), F32),
            pltpu.VMEM((chunk_count, 8, token_count), F32),
            pltpu.VMEM((chunk_count, 8, token_count), F32),
            pltpu.VMEM((HALO + token_count, CHUNK), F32),
            pltpu.VMEM((token_count, CHUNK), BF16),
            pltpu.VMEM((token_count // GROUP, GROUP, GROUP), BF16),
            pltpu.VMEM((token_count // GROUP, GROUP, GROUP), BF16),
            pltpu.VMEM((token_count // GROUP, GROUP, GROUP), F32),
            pltpu.VMEM((token_count // GROUP, GROUP, CHUNK), F32),
            pltpu.VMEM((token_count // GROUP, GROUP, CHUNK), BF16),
            pltpu.VMEM((token_count, CHUNK), F32),
            pltpu.VMEM((token_count, CHUNK), F32),
            pltpu.VMEM((chunk_count, GROUP, CHUNK), BF16),
            pltpu.VMEM((chunk_count, GROUP, CHUNK), BF16),
            pltpu.VMEM((token_count, CHUNK), BF16),
            pltpu.VMEM((chunk_count, positions, CHUNK), BF16),
            pltpu.SemaphoreType.DMA((slab_count, hops[0])),
            pltpu.SemaphoreType.DMA((slab_count, hops[0])),
            pltpu.SemaphoreType.DMA((slab_count, hops[1])),
            pltpu.SemaphoreType.DMA((slab_count, hops[1])),
            pltpu.SemaphoreType.DMA((SPLIT, max(planes - 1, 1))),
            pltpu.SemaphoreType.DMA((SPLIT, max(planes - 1, 1))),
            pltpu.SemaphoreType.DMA((slab_count,)),
            pltpu.SemaphoreType.DMA((slab_count,)),
            pltpu.SemaphoreType.DMA,
            pltpu.SemaphoreType.DMA,
            pltpu.SemaphoreType.DMA((chunk_count,)),
            pltpu.SemaphoreType.DMA((chunk_count,)),
            pltpu.SemaphoreType.DMA((chunk_count, hops[2])),
            pltpu.SemaphoreType.DMA((chunk_count, hops[2])),
            pltpu.SemaphoreType.DMA((chunk_count,)),
            pltpu.SemaphoreType.DMA((block_count,)),
            pltpu.SemaphoreType.DMA((slab_count,)),
            pltpu.SemaphoreType.DMA((7,)),
        ],
        compiler_params=pltpu.CompilerParams(
            collective_id=0, has_side_effects=True, vmem_limit_bytes=58 * 1024 * 1024
        ),
        name="projected_scan",
    )(
        tokens[0],
        in_gain.reshape(1, width),
        in_weight,
        conv_weight,
        conv_bias,
        log_decay[0],
        skip.reshape(1, heads),
        out_gain.reshape(1, inner),
        scan_order.reshape(1, positions),
    )
    return regrouped[None]


def solution(mesh):
    dp_count, seq_count = mesh.shape["dp"], mesh.shape["seq"]
    x_count = 2 ** (int(math.log2(dp_count)) // 2)
    while dp_count % x_count:
        x_count //= 2
    sizes = (dp_count // x_count, x_count, 2 if seq_count % 2 == 0 else 1, seq_count)
    in_specs = (
        P("dp", "seq", None),
        P(),
        P("dp", None),
        P(),
        P(),
        P("dp", None, "seq"),
        P(),
        P(),
        P(),
    )
    return jax.shard_map(
        functools.partial(on_device, sizes),
        mesh=mesh,
        in_specs=in_specs,
        out_specs=P("dp", "seq", None),
        check_vma=False,
    )
```
